128 devices in a mesh: gx: 8 (over x, core), gy: 16 (over y, z).
Axes of the slice: x: 4, y: 4, z: 4, core: 2. Of those that a mesh axis runs over, the one named last changes fastest.
Arguments:
- values: float32 [32768, 128], P(('gx', 'gy')), may hold values from -6 to 6
- noise: float32 [32768, 128], P(('gx', 'gy')), may hold values from 0.1 to 1
- fractions: float32 [3, 32768, 128], P(None, ('gx', 'gy')), may hold values from 0 to 1
- cell_xy: int32 [2, 32768, 128], P(None, ('gx', 'gy')), may hold values from 0 to 7
- cell_z: int32 [32768, 128], P(('gx', 'gy')), may hold values from 0 to 255
- tile_grid: int32 [32768], P(('gx', 'gy')), may hold values from 0 to 31
- counts: int32 [32768], P(('gx', 'gy')), may hold values from 1 to 128, as said below
- rate_x: float32 [512], replicated, may hold values from 0.01 to 4
- rate_y: float32 [512], replicated, may hold values from 0.01 to 4
- rate_z: float32 [256], replicated, may hold values from 0.01 to 4
Outputs:
- product: float32 [32768, 128], P(('gx', 'gy'))
The draws below stay inside these ranges and needn't reach their ends.
Inputs may be any that keep to these rules, and one draw needn't show every extreme that they name: `counts`: every fifth point tile, counted from tile 0, is full. `tile_grid`: A point tile's grid tile is numbered within its own device's block of the grid.
All inputs are finite; a program needn't handle non-finite values.
Results may differ from the reference program's by a relative error of at most 0.00005.
Values sent between devices are 32-bit elements; how exact they have to be, the bound alone decides.
No kernel may reach another device: no remote copies, remote signals or barrier semaphores. Data moves between devices by JAX's collectives and lax.ppermute only.
A program may use at most 128 MiB of HBM per device.

```python
import math
import jax
import jax.numpy as jnp
import numpy as np

NX = 512
NY = 512
NZ = 256
TILE = 8
PTS = 128
TILES_DEV = 256
TILES = 32768
GT_DEV = 32
N_GX = 8
N_GY = 16


def draw_counts(key, part):
    key = jax.random.fold_in(key, 7)
    drawn = jax.random.randint(key, (TILES,), 1, PTS + 1)
    slot_number = jnp.arange(TILES, dtype=jnp.int32)
    return jnp.where(slot_number % 5 == 0, PTS, drawn).astype(jnp.int32)


def touch_ends(result, rng, low, top_value):
    longest = result.shape.index(max(result.shape))
    spots = []
    for shift in (0, 1):
        where = [jax.random.randint(jax.random.fold_in(rng, axis), (), 0, length) for axis, length in enumerate(result.shape)]
        where[longest] = (where[longest] + shift) % result.shape[longest]
        spots.append(tuple(where))
    return result.at[spots[0]].set(low).at[spots[1]].set(top_value)


def shard_levels(rng, dims, cuts, least, high):
    def one(axis_at, parts):
        draws = jax.random.uniform(jax.random.fold_in(jax.random.fold_in(rng, 6), axis_at), (parts,), jnp.float32, least / len(cuts), high / len(cuts))
        return jnp.repeat(jnp.exp(draws), dims[axis_at] // parts).reshape((-1,) + (1,) * (len(dims) - axis_at - 1))

    factor_of = one(*cuts[0])
    for cut in cuts[1:]:
        factor_of = factor_of * one(*cut)
    return factor_of


def rank_bounds(number_of, lean):
    loads = [(1 << 20) // math.isqrt(rank ** lean) + 1 for rank in range(1, number_of + 1)]
    deviation = 1 + sum(loads) // (1 << 30)
    return np.cumsum(np.array([max(1, weight // deviation) for weight in loads]))


def ranked(rng, shape, number_of, lean):
    table = rank_bounds(number_of, lean)
    pick = jax.random.randint(jax.random.fold_in(rng, 1), shape, 0, int(table[number_of - 1]))
    standing = jnp.searchsorted(jnp.asarray(table, jnp.int32), pick, side="right")
    return jax.random.permutation(jax.random.fold_in(rng, 2), number_of)[standing].astype(jnp.int32)


def normal_values(key, shape, scale, limit, shards=(), kind=jnp.bfloat16):
    entries = scale * jax.random.normal(key, shape, jnp.float32)
    if shards:
        entries = entries * shard_levels(key, shape, shards, -0.22, 0.18)
    return jnp.clip(entries, -limit, limit).astype(kind)


def setup_inputs(seed: int = 0) -> dict:
    key_list = jax.random.split(jax.random.key(seed), 11)
    return {
        "values": normal_values(key_list[0], (TILES, PTS), 1.0, 6.0, ((0, 128),), jnp.float32),
        "noise": jnp.clip(jnp.exp(math.log(1.0) - 2.3025851 * jax.random.uniform(key_list[1], (TILES, PTS), jnp.float32) ** shard_levels(key_list[1], (TILES, PTS), ((0, 128),), -0.2, 0.2)), 0.1, 1.0),
        "fractions": jnp.clip(1.0 * jax.random.uniform(key_list[2], (3, TILES, PTS), jnp.float32) ** shard_levels(key_list[2], (3, TILES, PTS), ((1, 128),), -0.2, 0.2), 0.0, 1.0),
        "cell_xy": touch_ends(jax.random.randint(key_list[3], (2, TILES, PTS), 0, TILE), jax.random.fold_in(key_list[3], 1), 0, TILE - 1).astype(jnp.int32),
        "cell_z": touch_ends(jax.random.randint(key_list[4], (TILES, PTS), 0, NZ), jax.random.fold_in(key_list[4], 1), 0, NZ - 1).astype(jnp.int32),
        "tile_grid": touch_ends(ranked(key_list[5], (TILES,), GT_DEV, 2), jax.random.fold_in(key_list[5], 3), 0, GT_DEV - 1).astype(jnp.int32),
        "counts": draw_counts(jax.random.fold_in(key_list[10], 71), 0),
        "rate_x": jnp.clip(jnp.exp(jax.random.uniform(key_list[7], (NX,), jnp.float32, math.log(0.01), math.log(4.0))), 0.01, 4.0),
        "rate_y": jnp.clip(jnp.exp(jax.random.uniform(key_list[8], (NY,), jnp.float32, math.log(0.01), math.log(4.0))), 0.01, 4.0),
        "rate_z": jnp.clip(jnp.exp(jax.random.uniform(key_list[9], (NZ,), jnp.float32, math.log(0.01), math.log(4.0))), 0.01, 4.0),
    }


def cubic_taps(fraction):
    square = fraction * fraction
    cubed = square * fraction
    return (-0.5 * cubed + square - 0.5 * fraction,
            1.5 * cubed - 2.5 * square + 1.0,
            -1.5 * cubed + 2.0 * square + 0.5 * fraction,
            0.5 * cubed - 0.5 * square)


def hartley(grid_field, axis_number):
    spectrum = jnp.fft.fft(grid_field, axis=axis_number)
    return jnp.real(spectrum) - jnp.imag(spectrum)


def reference(values, noise, fractions, cell_xy, cell_z, tile_grid, counts, rate_x, rate_y, rate_z):
    cells_x = NX // N_GX
    cells_y = NY // N_GY
    rows_y = cells_y // TILE
    owner_dev = jnp.arange(TILES, dtype=jnp.int32) // TILES_DEV
    anchor_x = (owner_dev // N_GY) * cells_x + (tile_grid // rows_y) * TILE
    anchor_y = (owner_dev % N_GY) * cells_y + (tile_grid % rows_y) * TILE
    is_live = jnp.arange(PTS, dtype=jnp.int32)[None, :] < counts[:, None]
    source = jnp.where(is_live, values, 0.0)
    base_x = anchor_x[:, None] + cell_xy[0] - 1
    base_y = anchor_y[:, None] + cell_xy[1] - 1
    base_z = cell_z - 1
    taps_x = cubic_taps(fractions[0])
    taps_y = cubic_taps(fractions[1])
    taps_z = cubic_taps(fractions[2])
    spread = jnp.zeros((NX, NY, NZ), jnp.float32)
    for tap_x in range(4):
        index_x = (base_x + tap_x) % NX
        for tap_y in range(4):
            index_y = (base_y + tap_y) % NY
            weight_xy = taps_x[tap_x] * taps_y[tap_y]
            for tap_z in range(4):
                index_z = (base_z + tap_z) % NZ
                spread = spread.at[index_x, index_y, index_z].add(weight_xy * taps_z[tap_z] * source)
    coeffs = hartley(hartley(hartley(spread, 0), 1), 2)
    denom = 1.0 + rate_x[:, None, None] + rate_y[None, :, None] + rate_z[None, None, :]
    weighted = coeffs * (4.0 / (denom * denom))
    smooth = hartley(hartley(hartley(weighted, 0), 1), 2) / (NX * NY * NZ)
    sampled = jnp.zeros((TILES, PTS), jnp.float32)
    for tap_x in range(4):
        index_x = (base_x + tap_x) % NX
        for tap_y in range(4):
            index_y = (base_y + tap_y) % NY
            weight_xy = taps_x[tap_x] * taps_y[tap_y]
            for tap_z in range(4):
                index_z = (base_z + tap_z) % NZ
                sampled = sampled + weight_xy * taps_z[tap_z] * smooth[index_x, index_y, index_z]
    return jnp.where(is_live, noise * values + sampled, 0.0)
```

```python
import math

import jax
import jax.numpy as jnp
import ml_dtypes
import numpy as np
from jax import lax
from jax.experimental import pallas as pl
from jax.experimental.pallas import tpu as pltpu
from jax.sharding import PartitionSpec as P

NX, NY, NZ = 512, 512, 256
TILE = 8
PTS = 128
RX, RY = 8, 16
DEVS = RX * RY
BX, BY = NX // RX, NY // RY
GROW = BY // TILE
EY = BY + 3
SY, SX = 36, 72
BOX = 11
BLK = 40
HALO = ((0, -1), (65, 64), (66, 65))
CHUNK = 128

BF = jnp.bfloat16
F32 = jnp.float32
NN = (((1,), (0,)), ((), ()))
NT = (((1,), (1,)), ((), ()))


def halves(table):
    table = np.asarray(table, np.float32)
    high = table.astype(ml_dtypes.bfloat16)
    low = (table - high.astype(np.float32)).astype(ml_dtypes.bfloat16)
    return high, low


def cas(rows, columns, length):
    phase = np.outer(np.asarray(rows, np.int64), np.asarray(columns, np.int64)) % length
    angle = phase * (2.0 * math.pi / length)
    return np.cos(angle) + np.sin(angle)


def tables():
    cas_z = cas(np.arange(NZ), np.arange(NZ), NZ)
    cas_x = cas(np.arange(NX), np.arange(NX), NX)
    line = np.arange(EY) - 1
    full_y = cas(np.arange(NY), (np.arange(RY)[:, None] * BY + line[None, :]).reshape(-1) % NY, NY)
    full_y = full_y.reshape(NY, RY, EY)
    rows_y = np.zeros((NY, RY, BLK))
    rows_y[:, :, :EY] = full_y
    rows_y = rows_y.reshape(NY, RY * BLK)
    edge_y = np.zeros((NY, RY, 64))
    edge_y[:, :, :EY] = full_y
    edge_y = edge_y.reshape(NY, RY * 64)
    edge_x = cas(
        np.concatenate([np.arange(RX) * BX + offset for _, offset in HALO]) % NX, np.arange(NX), NX
    )
    edge_two = np.zeros((2, 48, NX))
    edge_two[0, :24] = edge_x
    edge_two[1, 24:] = edge_x
    return {
        "z": halves(cas_z),
        "x": halves(cas_x),
        "y": halves(rows_y),
        "yt": halves(rows_y.T),
        "ey": halves(edge_y),
        "ex2": halves(edge_two),
        "ex": halves(edge_x),
    }


def split(value):
    high = value.astype(BF)
    return high, (value - high.astype(F32)).astype(BF)


def mm(a, b, dims=NN):
    return lax.dot_general(a, b, dims, preferred_element_type=F32)


def mm3(a, b, dims=NN):
    return mm(a[0], b[0], dims) + (mm(a[0], b[1], dims) + mm(a[1], b[0], dims))


def cubic_taps(fraction):
    square = fraction * fraction
    cubed = square * fraction
    return (
        -0.5 * cubed + square - 0.5 * fraction,
        1.5 * cubed - 2.5 * square + 1.0,
        -1.5 * cubed + 2.0 * square + 0.5 * fraction,
        0.5 * cubed - 0.5 * square,
    )


def low_lanes(shape):
    return lax.broadcasted_iota(jnp.int32, shape, 1) < 64


def swap(a, b):
    low = low_lanes(a.shape)
    return (
        jnp.where(low, a, pltpu.roll(b, 64, 1)),
        jnp.where(low, pltpu.roll(a, 64, 1), b),
    )


def fill_taps(frac_ref, taps_ref):
    tiles = frac_ref.shape[1]

    def step(i, carry):
        rows = pl.ds(pl.multiple_of(i * 8, 8), 8)
        for axis in range(3):
            for offset, tap in enumerate(cubic_taps(frac_ref[axis, rows, :])):
                taps_ref[axis * 4 + offset, rows, :] = tap
        return carry

    lax.fori_loop(0, tiles // 8, step, 0)


def window(start, taps, length):
    delta = lax.broadcasted_iota(jnp.int32, (length, PTS), 0) - start
    weights = jnp.where(delta == 0, taps[0], 0.0)
    for offset in range(1, 4):
        weights = jnp.where(delta == offset, taps[offset], weights)
    return weights


def column(start, taps):
    delta = (lax.broadcasted_iota(jnp.int32, (NZ, PTS), 0) - (start - 1)) & (NZ - 1)
    weights = jnp.where(delta == 0, taps[0], 0.0)
    for offset in range(1, 4):
        weights = jnp.where(delta == offset, taps[offset], weights)
    return weights


def tile_rows(t, taps_ref, xy_ref, z_ref):
    row = pl.ds(t, 1)
    taps = [taps_ref[k, row, :] for k in range(12)]
    return taps, xy_ref[0, row, :], xy_ref[1, row, :], z_ref[row, :]


def spread_kernel(
    grid_ref, counts_ref, val_ref, frac_ref, xy_ref, z_ref, tzh_ref, tzl_ref, out_ref, taps_ref, pad_ref
):
    tiles = val_ref.shape[0]
    fill_taps(frac_ref, taps_ref)
    pad_ref[...] = jnp.zeros_like(pad_ref)
    slots = lax.broadcasted_iota(jnp.int32, (1, PTS), 1)

    def step(t, carry):
        taps, cell_x, cell_y, cell_z = tile_rows(t, taps_ref, xy_ref, z_ref)
        source = jnp.where(slots < counts_ref[t], val_ref[pl.ds(t, 1), :], 0.0)
        wide_x = window(cell_x, taps[0:4], 16)
        wide_y = window(cell_y, [tap * source for tap in taps[4:8]], 16)
        plane = jnp.concatenate([wide_y[q : q + 1] * wide_x for q in range(BOX)], 0)
        plane = split(plane)
        col = split(column(cell_z, taps[8:12]))
        box = mm3(plane, col, NT)
        g = grid_ref[t]
        gx = g // GROW
        gy = g - gx * GROW
        place = pl.ds(pl.multiple_of(gx * TILE, TILE), 16)
        for q in range(BOX):
            pad_ref[gy * TILE + q, place, :] += box[q * 16 : q * 16 + 16]
        return carry

    lax.fori_loop(0, tiles, step, 0)

    table = (tzh_ref[...], tzl_ref[...])

    def put(rows, first, second):
        turned = mm3(table, split(rows), NT)
        a, b = swap(turned[:DEVS], turned[DEVS:])
        out_ref[pl.ds(first, DEVS, stride=BLK), :] = a
        if second is not None:
            out_ref[pl.ds(second, DEVS, stride=BLK), :] = b

    for pair in range(SY // 2):
        y = 2 * pair
        rows = jnp.concatenate([pad_ref[y, 1:65, :], pad_ref[y + 1, 1:65, :]], 0)
        put(rows, y, y + 1 if y + 1 < EY else None)
    edges = [
        jnp.concatenate([pad_ref[:, at, :], jnp.zeros((64 - SY, NZ), F32)], 0) for at, _ in HALO
    ]
    put(jnp.concatenate([edges[0], edges[1]], 0), EY, EY + 1)
    put(jnp.concatenate([edges[2], jnp.zeros((64, NZ), F32)], 0), EY + 2, EY + 3)
    out_ref[pl.ds(BLK - 1, DEVS, stride=BLK), :] = jnp.zeros((DEVS, 128), F32)


def filter_kernel(
    dev_ref, rz_ref, rx_ref, ry_ref, in_ref, xh_ref, xl_ref, yh_ref, yl_ref, yth_ref, ytl_ref, eyh_ref, eyl_ref,
    ex2h_ref, ex2l_ref, exh_ref, exl_ref, out_ref,
    th_ref, tl_ref, eh_ref, el_ref, wh_ref, wl_ref, uh_ref, ul_ref, ry2_ref,
):
    rows = RY * BLK
    parts = ([], [])
    for j in range(RY // 2):
        load = [
            jnp.concatenate(
                [
                    in_ref[pl.ds((2 * j + i) * BLK + EY + col, RX, stride=rows), :]
                    for col in range(3)
                ],
                0,
            )
            for i in range(2)
        ]
        a, b = swap(load[0], load[1])
        parts[0].append(a)
        parts[1].append(b)
    edge = split(jnp.concatenate([jnp.concatenate(p, 1) for p in parts], 0))

    def edges(i, carry):
        at = pl.ds(pl.multiple_of(i * CHUNK, CHUNK), CHUNK)
        high, low = split(mm3((eyh_ref[at, :], eyl_ref[at, :]), edge, NT))
        eh_ref[at, :] = high
        el_ref[at, :] = low
        return carry

    lax.fori_loop(0, NY // CHUNK, edges, 0)

    for j in range(RX // 2):
        pair = split(
            jnp.concatenate(
                [in_ref[2 * j * rows : (2 * j + 1) * rows, :], in_ref[(2 * j + 1) * rows : (2 * j + 2) * rows, :]], 1
            )
        )

        def forward_y(i, carry):
            at = pl.ds(pl.multiple_of(i * CHUNK, CHUNK), CHUNK)
            turned = mm3((yh_ref[at, :], yl_ref[at, :]), pair)
            for z, part in enumerate(swap(turned[:, :128], turned[:, 128:])):
                high, low = split(part)
                th_ref[z, at, 128 * j : 128 * (j + 1)] = high
                tl_ref[z, at, 128 * j : 128 * (j + 1)] = low
            return carry

        lax.fori_loop(0, NY // CHUNK, forward_y, 0)

    ry2_ref[...] = jnp.transpose(jnp.broadcast_to(ry_ref[...], (128, NY)))
    dev = dev_ref[0]
    scale = 4.0 / (NX * NY * NZ)

    def middle(i, carry):
        at = pl.ds(pl.multiple_of(i * CHUNK, CHUNK), CHUNK)
        table = (xh_ref[...], xl_ref[...])
        back = []
        for z in range(2):
            coeffs = mm3((th_ref[z, at, :], tl_ref[z, at, :]), table) + mm3(
                (eh_ref[at, :], el_ref[at, :]), (ex2h_ref[z], ex2l_ref[z])
            )
            rate = 1.0 + rz_ref[dev + z * DEVS]
            weighted = []
            for k in range(NX // 128):
                lanes = slice(128 * k, 128 * (k + 1))
                denom = ry2_ref[at, :] + (rx_ref[:, lanes] + rate)
                weighted.append(coeffs[:, lanes] * (scale / (denom * denom)))
            weighted = split(jnp.concatenate(weighted, 1))
            wh_ref[z, at, :] = weighted[0]
            wl_ref[z, at, :] = weighted[1]
            back.append(mm3(weighted, table))
        for k in range(NX // 128):
            lanes = slice(128 * k, 128 * (k + 1))
            for n, part in enumerate(swap(back[0][:, lanes], back[1][:, lanes])):
                high, low = split(part)
                uh_ref[at, (2 * k + n) * 128 : (2 * k + n + 1) * 128] = high
                ul_ref[at, (2 * k + n) * 128 : (2 * k + n + 1) * 128] = low
        return carry

    lax.fori_loop(0, NY // CHUNK, middle, 0)

    for j in range(RX // 2):
        lanes = slice(256 * j, 256 * (j + 1))
        field = (uh_ref[:, lanes], ul_ref[:, lanes])

        def backward_y(i, carry):
            at = pl.ds(pl.multiple_of(i * 160, 160), 160)
            turned = mm3((yth_ref[at, :], ytl_ref[at, :]), field)
            for n in range(2):
                out_ref[pl.ds(pl.multiple_of((2 * j + n) * rows + i * 160, 160), 160), :] = turned[
                    :, 128 * n : 128 * (n + 1)
                ]
            return carry

        lax.fori_loop(0, rows // 160, backward_y, 0)

    edge_x = (exh_ref[...], exl_ref[...])
    tall = split(
        jnp.concatenate([mm3(edge_x, (wh_ref[z], wl_ref[z]), NT) for z in range(2)], 0)
    )
    for j in range(RY // 2):
        lanes = slice(128 * j, 128 * (j + 1))
        wide = mm3(tall, (eyh_ref[:, lanes], eyl_ref[:, lanes]))
        for n, part in enumerate(swap(wide[:24], wide[24:])):
            for col in range(3):
                out_ref[pl.ds((2 * j + n) * BLK + EY + col, RX, stride=rows), :] = part[
                    8 * col : 8 * col + 8
                ]


def sample_kernel(
    grid_ref, counts_ref, val_ref, noise_ref, frac_ref, xy_ref, z_ref, in_ref, tzh_ref, tzl_ref, out_ref,
    taps_ref, pad_ref, boxh_ref, boxl_ref,
):
    tiles = val_ref.shape[0]
    fill_taps(frac_ref, taps_ref)
    table = (tzh_ref[...], tzl_ref[...])

    def get(first, second):
        a = in_ref[pl.ds(first, DEVS, stride=BLK), :]
        b = in_ref[pl.ds(second, DEVS, stride=BLK), :]
        turned = jnp.concatenate(swap(a, b), 0)
        return mm3(split(jnp.transpose(turned)), table)

    for pair in range(SY // 2):
        y = 2 * pair
        rows = get(y, y + 1)
        pad_ref[y, 1:65, :] = rows[:64]
        pad_ref[y + 1, 1:65, :] = rows[64:]
    for first, at in ((EY, (0, 1)), (EY + 2, (2,))):
        rows = get(first, first + 1)
        for n, col in enumerate(at):
            pad_ref[:, HALO[col][0], :] = rows[64 * n : 64 * n + SY]
    pad_ref[:, 67:72, :] = jnp.zeros((SY, 5, NZ), F32)
    for gx in range(BX // TILE):
        for y in range(SY):
            high, low = split(pad_ref[y, TILE * gx : TILE * gx + 16, :])
            boxh_ref[gx, y] = high
            boxl_ref[gx, y] = low

    slots = lax.broadcasted_iota(jnp.int32, (1, PTS), 1)

    def step(t, carry):
        taps, cell_x, cell_y, cell_z = tile_rows(t, taps_ref, xy_ref, z_ref)
        wide_x = window(cell_x, taps[0:4], 16)
        wide_y = window(cell_y, taps[4:8], 16)
        col = split(column(cell_z, taps[8:12]))
        g = grid_ref[t]
        gx = g // GROW
        gy = g - gx * GROW
        place = pl.ds(gy * TILE, BOX)
        high = boxh_ref[gx, place].reshape(BOX * 16, NZ)
        low = boxl_ref[gx, place].reshape(BOX * 16, NZ)
        along = mm(high, jnp.concatenate(col, 1))
        along = along[:, :PTS] + along[:, PTS:] + mm(low, col[0])
        total = wide_y[0:1] * along[0:16]
        for q in range(1, BOX):
            total = total + wide_y[q : q + 1] * along[16 * q : 16 * q + 16]
        sampled = jnp.sum(total * wide_x, axis=0, keepdims=True)
        row = pl.ds(t, 1)
        out_ref[row, :] = jnp.where(
            slots < counts_ref[t], noise_ref[row, :] * val_ref[row, :] + sampled, 0.0
        )
        return carry

    lax.fori_loop(0, tiles, step, 0)


def body(values, noise, fractions, cell_xy, cell_z, tile_grid, counts, rate_x, rate_y, rate_z):
    tiles = values.shape[0]
    tab = {name: (jnp.asarray(pair[0]), jnp.asarray(pair[1])) for name, pair in tables().items()}
    vmem = pl.BlockSpec(memory_space=pltpu.VMEM)
    smem = pl.BlockSpec(memory_space=pltpu.SMEM)
    limit = pltpu.CompilerParams(vmem_limit_bytes=56 << 20)
    exchange = jax.ShapeDtypeStruct((DEVS * BLK, 128), F32)

    sent = pl.pallas_call(
        spread_kernel,
        out_shape=exchange,
        in_specs=[smem] * 2 + [vmem] * 6,
        out_specs=vmem,
        scratch_shapes=[pltpu.VMEM((12, tiles, PTS), F32), pltpu.VMEM((SY, SX, NZ), F32)],
        compiler_params=limit,
    )(tile_grid, counts, values, fractions, cell_xy, cell_z, *tab["z"])

    def regroup(array):
        array = array.reshape(DEVS, BLK, 128)
        array = lax.all_to_all(array, ("gx", "gy"), split_axis=0, concat_axis=0, tiled=True)
        return array.reshape(DEVS * BLK, 128)

    planes = regroup(sent)
    dev = (lax.axis_index("gx") * RY + lax.axis_index("gy")).astype(jnp.int32).reshape(1)
    filtered = pl.pallas_call(
        filter_kernel,
        out_shape=exchange,
        in_specs=[smem] * 2 + [vmem] * 15,
        out_specs=vmem,
        scratch_shapes=[
            pltpu.VMEM((2, NY, NX), BF),
            pltpu.VMEM((2, NY, NX), BF),
            pltpu.VMEM((NY, 48), BF),
            pltpu.VMEM((NY, 48), BF),
            pltpu.VMEM((2, NY, NX), BF),
            pltpu.VMEM((2, NY, NX), BF),
            pltpu.VMEM((NY, 2 * NX), BF),
            pltpu.VMEM((NY, 2 * NX), BF),
            pltpu.VMEM((NY, 128), F32),
        ],
        compiler_params=limit,
    )(
        dev, rate_z, rate_x.reshape(1, NX), rate_y.reshape(1, NY), planes,
        *tab["x"], *tab["y"], *tab["yt"], *tab["ey"], *tab["ex2"], *tab["ex"],
    )
    smooth = regroup(filtered)

    return pl.pallas_call(
        sample_kernel,
        out_shape=jax.ShapeDtypeStruct((tiles, PTS), F32),
        in_specs=[smem] * 2 + [vmem] * 8,
        out_specs=vmem,
        scratch_shapes=[
            pltpu.VMEM((12, tiles, PTS), F32),
            pltpu.VMEM((SY, SX, NZ), F32),
            pltpu.VMEM((BX // TILE, SY, 16, NZ), BF),
            pltpu.VMEM((BX // TILE, SY, 16, NZ), BF),
        ],
        compiler_params=limit,
    )(tile_grid, counts, values, noise, fractions, cell_xy, cell_z, smooth, *tab["z"])


def solution(mesh):
    points = P(("gx", "gy"), None)
    triple = P(None, ("gx", "gy"), None)
    flat = P(("gx", "gy"))
    in_specs = (points, points, triple, triple, points, flat, flat, P(), P(), P())
    return jax.shard_map(body, mesh=mesh, in_specs=in_specs, out_specs=points, check_vma=False)
```

```python
import math

import jax
import jax.numpy as jnp
import ml_dtypes
import numpy as np
from jax import lax
from jax.experimental import pallas as pl
from jax.experimental.pallas import tpu as pltpu
from jax.sharding import PartitionSpec as P

NX, NY, NZ = 512, 512, 256
TILE = 8
PTS = 128
RX, RY = 8, 16
DEVS = RX * RY
BX, BY = NX // RX, NY // RY
GROW = BY // TILE
EY = BY + 3
SY, SX = 36, 72
BOX = 11
BLK = 40
HALO = ((0, -1), (65, 64), (66, 65))
CHUNK = 256

BF = jnp.bfloat16
F32 = jnp.float32
NN = (((1,), (0,)), ((), ()))
NT = (((1,), (1,)), ((), ()))


def halves(table):
    table = np.asarray(table, np.float32)
    high = table.astype(ml_dtypes.bfloat16)
    low = (table - high.astype(np.float32)).astype(ml_dtypes.bfloat16)
    return high, low


def cas(rows, columns, length):
    phase = np.outer(np.asarray(rows, np.int64), np.asarray(columns, np.int64)) % length
    angle = phase * (2.0 * math.pi / length)
    return np.cos(angle) + np.sin(angle)


def tables():
    cas_z = cas(np.arange(NZ), np.arange(NZ), NZ)
    cas_x = cas(np.arange(NX), np.arange(NX), NX)
    line = np.arange(EY) - 1
    full_y = cas(np.arange(NY), (np.arange(RY)[:, None] * BY + line[None, :]).reshape(-1) % NY, NY)
    full_y = full_y.reshape(NY, RY, EY)
    rows_y = np.zeros((NY, RY, BLK))
    rows_y[:, :, :EY] = full_y
    rows_y = rows_y.reshape(NY, RY * BLK)
    edge_y = np.zeros((NY, RY, 64))
    edge_y[:, :, :EY] = full_y
    edge_y = edge_y.reshape(NY, RY * 64)
    edge_x = cas(
        np.concatenate([np.arange(RX) * BX + offset for _, offset in HALO]) % NX, np.arange(NX), NX
    )
    edge_two = np.zeros((2, 48, NX))
    edge_two[0, :24] = edge_x
    edge_two[1, 24:] = edge_x
    return {
        "z": halves(cas_z),
        "x": halves(cas_x),
        "y": halves(rows_y),
        "yt": halves(rows_y.T),
        "ey": halves(edge_y),
        "ex2": halves(edge_two),
        "ex": halves(edge_x),
    }


def split(value):
    high = value.astype(BF)
    return high, (value - high.astype(F32)).astype(BF)


def mm(a, b, dims=NN):
    return lax.dot_general(a, b, dims, preferred_element_type=F32)


def mm3(a, b, dims=NN):
    return mm(a[0], b[0], dims) + (mm(a[0], b[1], dims) + mm(a[1], b[0], dims))


def cubic_taps(fraction):
    square = fraction * fraction
    cubed = square * fraction
    return (
        -0.5 * cubed + square - 0.5 * fraction,
        1.5 * cubed - 2.5 * square + 1.0,
        -1.5 * cubed + 2.0 * square + 0.5 * fraction,
        0.5 * cubed - 0.5 * square,
    )


def low_lanes(shape):
    return lax.broadcasted_iota(jnp.int32, shape, 1) < 64


def swap(a, b):
    low = low_lanes(a.shape)
    return (
        jnp.where(low, a, pltpu.roll(b, 64, 1)),
        jnp.where(low, pltpu.roll(a, 64, 1), b),
    )


def fill_taps(frac_ref, z_ref, taps_ref, cells_ref):
    tiles = frac_ref.shape[1]

    def step(i, carry):
        rows = pl.ds(pl.multiple_of(i * 8, 8), 8)
        for axis in range(2):
            for offset, tap in enumerate(cubic_taps(frac_ref[axis, rows, :])):
                taps_ref[axis * 4 + offset, rows, :] = tap
        for offset, tap in enumerate(cubic_taps(frac_ref[2, rows, :])):
            high, low = split(tap)
            cell = (z_ref[rows, :] + (offset - 1)) & (NZ - 1)
            taps_ref[8 + offset, rows, :] = cell.astype(F32)
            taps_ref[12 + offset, rows, :] = high.astype(F32)
            taps_ref[16 + offset, rows, :] = low.astype(F32)
        return carry

    lax.fori_loop(0, tiles // 8, step, 0)
    cells_ref[...] = lax.broadcasted_iota(jnp.int32, (NZ, PTS), 0).astype(F32).astype(BF)


def window(start, taps, length):
    delta = lax.broadcasted_iota(jnp.int32, (length, PTS), 0) - start
    weights = jnp.where(delta == 0, taps[0], 0.0)
    for offset in range(1, 4):
        weights = jnp.where(delta == offset, taps[offset], weights)
    return weights


def column(row, taps_ref, cells_ref):
    cells = cells_ref[...]
    high = low = jnp.zeros((NZ, PTS), BF)
    for k in range(4):
        hit = cells == taps_ref[8 + k, row, :].astype(BF)
        high = jnp.where(hit, taps_ref[12 + k, row, :].astype(BF), high)
        low = jnp.where(hit, taps_ref[16 + k, row, :].astype(BF), low)
    return high, low


def spread_kernel(
    grid_ref, counts_ref, val_ref, frac_ref, xy_ref, z_ref, tzh_ref, tzl_ref, out_ref,
    taps_ref, cells_ref, pad_ref,
):
    tiles = val_ref.shape[0]
    fill_taps(frac_ref, z_ref, taps_ref, cells_ref)
    pad_ref[...] = jnp.zeros_like(pad_ref)
    slots = lax.broadcasted_iota(jnp.int32, (1, PTS), 1)

    def step(t, carry):
        row = pl.ds(t, 1)
        taps = [taps_ref[k, row, :] for k in range(8)]
        source = jnp.where(slots < counts_ref[t], val_ref[row, :], 0.0)
        wide_x = window(xy_ref[0, row, :], taps[0:4], 16)
        wide_y = window(xy_ref[1, row, :], [tap * source for tap in taps[4:8]], 16)
        plane = jnp.concatenate([wide_y[q : q + 1] * wide_x for q in range(BOX)], 0)
        high, low = split(plane)
        col = column(row, taps_ref, cells_ref)
        box = mm(
            jnp.concatenate([high, low, high], 1), jnp.concatenate([col[0], col[0], col[1]], 1), NT
        )
        g = grid_ref[t]
        gx = g // GROW
        gy = g - gx * GROW
        place = pl.ds(pl.multiple_of(gx * TILE, TILE), 16)
        for q in range(BOX):
            pad_ref[gy * TILE + q, place, :] += box[q * 16 : q * 16 + 16]
        return carry

    lax.fori_loop(0, tiles, step, 0, unroll=16)

    table = (tzh_ref[...], tzl_ref[...])

    def put(rows, first, second):
        turned = mm3(table, split(rows), NT)
        a, b = swap(turned[:DEVS], turned[DEVS:])
        out_ref[pl.ds(first, DEVS, stride=BLK), :] = a
        if second is not None:
            out_ref[pl.ds(second, DEVS, stride=BLK), :] = b

    for pair in range(SY // 2):
        y = 2 * pair
        rows = jnp.concatenate([pad_ref[y, 1:65, :], pad_ref[y + 1, 1:65, :]], 0)
        put(rows, y, y + 1 if y + 1 < EY else None)
    edges = [
        jnp.concatenate([pad_ref[:, at, :], jnp.zeros((64 - SY, NZ), F32)], 0) for at, _ in HALO
    ]
    put(jnp.concatenate([edges[0], edges[1]], 0), EY, EY + 1)
    put(jnp.concatenate([edges[2], jnp.zeros((64, NZ), F32)], 0), EY + 2, EY + 3)
    out_ref[pl.ds(BLK - 1, DEVS, stride=BLK), :] = jnp.zeros((DEVS, 128), F32)


def filter_kernel(
    dev_ref, rz_ref, rx_ref, ry_ref, in_ref, xh_ref, xl_ref, yh_ref, yl_ref, yth_ref, ytl_ref, eyh_ref, eyl_ref,
    ex2h_ref, ex2l_ref, exh_ref, exl_ref, out_ref,
    th_ref, tl_ref, eh_ref, el_ref, wh_ref, wl_ref, uh_ref, ul_ref, ry2_ref,
):
    rows = RY * BLK
    parts = ([], [])
    for j in range(RY // 2):
        load = [
            jnp.concatenate(
                [
                    in_ref[pl.ds((2 * j + i) * BLK + EY + col, RX, stride=rows), :]
                    for col in range(3)
                ],
                0,
            )
            for i in range(2)
        ]
        a, b = swap(load[0], load[1])
        parts[0].append(a)
        parts[1].append(b)
    edge = split(jnp.concatenate([jnp.concatenate(p, 1) for p in parts], 0))

    def edges(i, carry):
        at = pl.ds(pl.multiple_of(i * CHUNK, CHUNK), CHUNK)
        high, low = split(mm3((eyh_ref[at, :], eyl_ref[at, :]), edge, NT))
        eh_ref[at, :] = high
        el_ref[at, :] = low
        return carry

    lax.fori_loop(0, NY // CHUNK, edges, 0, unroll=True)

    for j in range(RX // 2):
        pair = split(
            jnp.concatenate(
                [in_ref[2 * j * rows : (2 * j + 1) * rows, :], in_ref[(2 * j + 1) * rows : (2 * j + 2) * rows, :]], 1
            )
        )

        def forward_y(i, carry):
            at = pl.ds(pl.multiple_of(i * CHUNK, CHUNK), CHUNK)
            turned = mm3((yh_ref[at, :], yl_ref[at, :]), pair)
            for z, part in enumerate(swap(turned[:, :128], turned[:, 128:])):
                high, low = split(part)
                th_ref[z, at, 128 * j : 128 * (j + 1)] = high
                tl_ref[z, at, 128 * j : 128 * (j + 1)] = low
            return carry

        lax.fori_loop(0, NY // CHUNK, forward_y, 0, unroll=True)

    ry2_ref[...] = jnp.transpose(jnp.broadcast_to(ry_ref[...], (128, NY)))
    dev = dev_ref[0]
    scale = 4.0 / (NX * NY * NZ)

    def middle(i, carry):
        at = pl.ds(pl.multiple_of(i * CHUNK, CHUNK), CHUNK)
        table = (xh_ref[...], xl_ref[...])
        back = []
        for z in range(2):
            coeffs = mm3((th_ref[z, at, :], tl_ref[z, at, :]), table) + mm3(
                (eh_ref[at, :], el_ref[at, :]), (ex2h_ref[z], ex2l_ref[z])
            )
            rate = 1.0 + rz_ref[dev + z * DEVS]
            weighted = []
            for k in range(NX // 128):
                lanes = slice(128 * k, 128 * (k + 1))
                denom = ry2_ref[at, :] + (rx_ref[:, lanes] + rate)
                weighted.append(coeffs[:, lanes] * (scale / (denom * denom)))
            weighted = split(jnp.concatenate(weighted, 1))
            wh_ref[z, at, :] = weighted[0]
            wl_ref[z, at, :] = weighted[1]
            back.append(mm3(weighted, table))
        for k in range(NX // 128):
            lanes = slice(128 * k, 128 * (k + 1))
            for n, part in enumerate(swap(back[0][:, lanes], back[1][:, lanes])):
                high, low = split(part)
                uh_ref[at, (2 * k + n) * 128 : (2 * k + n + 1) * 128] = high
                ul_ref[at, (2 * k + n) * 128 : (2 * k + n + 1) * 128] = low
        return carry

    lax.fori_loop(0, NY // CHUNK, middle, 0, unroll=True)

    for j in range(RX // 2):
        lanes = slice(256 * j, 256 * (j + 1))
        field = (uh_ref[:, lanes], ul_ref[:, lanes])

        def backward_y(i, carry):
            at = pl.ds(pl.multiple_of(i * 160, 160), 160)
            turned = mm3((yth_ref[at, :], ytl_ref[at, :]), field)
            for n in range(2):
                out_ref[pl.ds(pl.multiple_of((2 * j + n) * rows + i * 160, 160), 160), :] = turned[
                    :, 128 * n : 128 * (n + 1)
                ]
            return carry

        lax.fori_loop(0, rows // 160, backward_y, 0, unroll=True)

    edge_x = (exh_ref[...], exl_ref[...])
    tall = split(
        jnp.concatenate([mm3(edge_x, (wh_ref[z], wl_ref[z]), NT) for z in range(2)], 0)
    )
    for j in range(RY // 2):
        lanes = slice(128 * j, 128 * (j + 1))
        wide = mm3(tall, (eyh_ref[:, lanes], eyl_ref[:, lanes]))
        for n, part in enumerate(swap(wide[:24], wide[24:])):
            for col in range(3):
                out_ref[pl.ds((2 * j + n) * BLK + EY + col, RX, stride=rows), :] = part[
                    8 * col : 8 * col + 8
                ]


def sample_kernel(
    grid_ref, counts_ref, val_ref, noise_ref, frac_ref, xy_ref, z_ref, in_ref, tzh_ref, tzl_ref, out_ref,
    taps_ref, cells_ref, pad_ref, boxh_ref, boxl_ref,
):
    tiles = val_ref.shape[0]
    fill_taps(frac_ref, z_ref, taps_ref, cells_ref)
    table = (tzh_ref[...], tzl_ref[...])

    def get(first, second):
        a = in_ref[pl.ds(first, DEVS, stride=BLK), :]
        b = in_ref[pl.ds(second, DEVS, stride=BLK), :]
        turned = jnp.concatenate(swap(a, b), 0)
        return mm3(split(jnp.transpose(turned)), table)

    for pair in range(SY // 2):
        y = 2 * pair
        rows = get(y, y + 1)
        pad_ref[y, 1:65, :] = rows[:64]
        pad_ref[y + 1, 1:65, :] = rows[64:]
    for first, at in ((EY, (0, 1)), (EY + 2, (2,))):
        rows = get(first, first + 1)
        for n, col in enumerate(at):
            pad_ref[:, HALO[col][0], :] = rows[64 * n : 64 * n + SY]
    pad_ref[:, 67:72, :] = jnp.zeros((SY, 5, NZ), F32)
    for gx in range(BX // TILE):
        for y in range(SY):
            high, low = split(pad_ref[y, TILE * gx : TILE * gx + 16, :])
            boxh_ref[gx, y] = high
            boxl_ref[gx, y] = low

    slots = lax.broadcasted_iota(jnp.int32, (1, PTS), 1)

    def step(t, carry):
        row = pl.ds(t, 1)
        taps = [taps_ref[k, row, :] for k in range(8)]
        wide_x = window(xy_ref[0, row, :], taps[0:4], 16)
        wide_y = window(xy_ref[1, row, :], taps[4:8], 16)
        col = column(row, taps_ref, cells_ref)
        g = grid_ref[t]
        gx = g // GROW
        gy = g - gx * GROW
        place = pl.ds(gy * TILE, BOX)
        high = boxh_ref[gx, place].reshape(BOX * 16, NZ)
        low = boxl_ref[gx, place].reshape(BOX * 16, NZ)
        along = mm(jnp.concatenate([high, low], 0), jnp.concatenate(col, 1))
        along = along[: BOX * 16, :PTS] + along[: BOX * 16, PTS:] + along[BOX * 16 :, :PTS]
        total = wide_y[0:1] * along[0:16]
        for q in range(1, BOX):
            total = total + wide_y[q : q + 1] * along[16 * q : 16 * q + 16]
        sampled = jnp.sum(total * wide_x, axis=0, keepdims=True)
        out_ref[row, :] = jnp.where(
            slots < counts_ref[t], noise_ref[row, :] * val_ref[row, :] + sampled, 0.0
        )
        return carry

    lax.fori_loop(0, tiles, step, 0, unroll=16)


def body(values, noise, fractions, cell_xy, cell_z, tile_grid, counts, rate_x, rate_y, rate_z):
    tiles = values.shape[0]
    tab = {name: (jnp.asarray(pair[0]), jnp.asarray(pair[1])) for name, pair in tables().items()}
    vmem = pl.BlockSpec(memory_space=pltpu.VMEM)
    smem = pl.BlockSpec(memory_space=pltpu.SMEM)
    limit = pltpu.CompilerParams(vmem_limit_bytes=56 << 20)
    exchange = jax.ShapeDtypeStruct((DEVS * BLK, 128), F32)

    sent = pl.pallas_call(
        spread_kernel,
        out_shape=exchange,
        in_specs=[smem] * 2 + [vmem] * 6,
        out_specs=vmem,
        scratch_shapes=[pltpu.VMEM((20, tiles, PTS), F32), pltpu.VMEM((NZ, PTS), BF), pltpu.VMEM((SY, SX, NZ), F32)],
        compiler_params=limit,
    )(tile_grid, counts, values, fractions, cell_xy, cell_z, *tab["z"])

    def regroup(array):
        array = array.reshape(DEVS, BLK, 128)
        array = lax.all_to_all(array, ("gx", "gy"), split_axis=0, concat_axis=0, tiled=True)
        return array.reshape(DEVS * BLK, 128)

    planes = regroup(sent)
    dev = (lax.axis_index("gx") * RY + lax.axis_index("gy")).astype(jnp.int32).reshape(1)
    filtered = pl.pallas_call(
        filter_kernel,
        out_shape=exchange,
        in_specs=[smem] * 2 + [vmem] * 15,
        out_specs=vmem,
        scratch_shapes=[
            pltpu.VMEM((2, NY, NX), BF),
            pltpu.VMEM((2, NY, NX), BF),
            pltpu.VMEM((NY, 48), BF),
            pltpu.VMEM((NY, 48), BF),
            pltpu.VMEM((2, NY, NX), BF),
            pltpu.VMEM((2, NY, NX), BF),
            pltpu.VMEM((NY, 2 * NX), BF),
            pltpu.VMEM((NY, 2 * NX), BF),
            pltpu.VMEM((NY, 128), F32),
        ],
        compiler_params=limit,
    )(
        dev, rate_z, rate_x.reshape(1, NX), rate_y.reshape(1, NY), planes,
        *tab["x"], *tab["y"], *tab["yt"], *tab["ey"], *tab["ex2"], *tab["ex"],
    )
    smooth = regroup(filtered)

    return pl.pallas_call(
        sample_kernel,
        out_shape=jax.ShapeDtypeStruct((tiles, PTS), F32),
        in_specs=[smem] * 2 + [vmem] * 8,
        out_specs=vmem,
        scratch_shapes=[
            pltpu.VMEM((20, tiles, PTS), F32),
            pltpu.VMEM((NZ, PTS), BF),
            pltpu.VMEM((SY, SX, NZ), F32),
            pltpu.VMEM((BX // TILE, SY, 16, NZ), BF),
            pltpu.VMEM((BX // TILE, SY, 16, NZ), BF),
        ],
        compiler_params=limit,
    )(tile_grid, counts, values, noise, fractions, cell_xy, cell_z, smooth, *tab["z"])


def solution(mesh):
    points = P(("gx", "gy"), None)
    triple = P(None, ("gx", "gy"), None)
    flat = P(("gx", "gy"))
    in_specs = (points, points, triple, triple, points, flat, flat, P(), P(), P())
    return jax.shard_map(body, mesh=mesh, in_specs=in_specs, out_specs=points, check_vma=False)
```

```python
import math

import jax
import jax.numpy as jnp
import ml_dtypes
import numpy as np
from jax import lax
from jax.experimental import pallas as pl
from jax.experimental.pallas import tpu as pltpu
from jax.sharding import PartitionSpec as P

NX, NY, NZ = 512, 512, 256
TILE = 8
PTS = 128
RX, RY = 8, 16
DEVS = RX * RY
BX, BY = NX // RX, NY // RY
GROW = BY // TILE
EY = BY + 3
SY, SX = 36, 72
BOX = 11
BLK = 40
HALO = ((0, -1), (65, 64), (66, 65))
CHUNK = 128

BF = jnp.bfloat16
F32 = jnp.float32
NN = (((1,), (0,)), ((), ()))
NT = (((1,), (1,)), ((), ()))


def halves(table):
    table = np.asarray(table, np.float32)
    high = table.astype(ml_dtypes.bfloat16)
    low = (table - high.astype(np.float32)).astype(ml_dtypes.bfloat16)
    return high, low


def cas(rows, columns, length):
    phase = np.outer(np.asarray(rows, np.int64), np.asarray(columns, np.int64)) % length
    angle = phase * (2.0 * math.pi / length)
    return np.cos(angle) + np.sin(angle)


def tables():
    half = np.arange(NX // 2)
    line = np.arange(EY) - 1
    full_y = cas(np.arange(NY), (np.arange(RY)[:, None] * BY + line[None, :]).reshape(-1) % NY, NY)
    full_y = full_y.reshape(NY, RY, EY)
    rows_y = np.zeros((NY // 2, RY, BLK))
    rows_y[:, :, :EY] = full_y[: NY // 2]
    rows_y = rows_y.reshape(NY // 2, RY * BLK // 2, 2)
    edge_y = np.zeros((NY, RY, 64))
    edge_y[:, :, :EY] = full_y
    edge_y = edge_y.reshape(NY, RY * 64)
    order = np.concatenate([2 * half, 2 * half + 1])
    edge_x = cas(np.concatenate([np.arange(RX) * BX + offset for _, offset in HALO]) % NX, order, NX)
    edge_two = np.zeros((2, 48, NX))
    edge_two[0, :24] = edge_x
    edge_two[1, 24:] = edge_x
    table_x = np.concatenate([cas(half, 2 * half, NX), cas(half, 2 * half + 1, NX)], 1)
    wide = np.concatenate([table_x, edge_two.reshape(96, NX), edge_x, np.zeros((8, NX))])
    return {
        "z": np.concatenate(halves(cas(np.arange(NZ), np.arange(NZ), NZ))),
        "x": np.stack(halves(wide)),
        "y": np.stack(halves(rows_y.transpose(2, 0, 1))),
        "yt": np.stack(halves(rows_y.transpose(2, 1, 0))),
        "ey": np.stack(halves(edge_y)),
    }


EX2 = NX // 2
EX = EX2 + 96


def split(value):
    high = value.astype(BF)
    return high, (value - high.astype(F32)).astype(BF)


def mm(a, b, dims=NN):
    return lax.dot_general(a, b, dims, preferred_element_type=F32)


def mm3(a, b, dims=NN):
    return mm(a[0], b[0], dims) + (mm(a[0], b[1], dims) + mm(a[1], b[0], dims))


def cubic_taps(fraction):
    square = fraction * fraction
    cubed = square * fraction
    return (
        -0.5 * cubed + square - 0.5 * fraction,
        1.5 * cubed - 2.5 * square + 1.0,
        -1.5 * cubed + 2.0 * square + 0.5 * fraction,
        0.5 * cubed - 0.5 * square,
    )


def low_lanes(shape):
    return lax.broadcasted_iota(jnp.int32, shape, 1) < 64


def swap(a, b):
    low = low_lanes(a.shape)
    return (
        jnp.where(low, a, pltpu.roll(b, 64, 1)),
        jnp.where(low, pltpu.roll(a, 64, 1), b),
    )


def fill_taps(frac_ref, z_ref, taps_ref):
    tiles = frac_ref.shape[1]

    def step(i, carry):
        rows = pl.ds(pl.multiple_of(i * 8, 8), 8)
        for axis in range(2):
            for offset, tap in enumerate(cubic_taps(frac_ref[axis, rows, :])):
                taps_ref[axis * 4 + offset, rows, :] = tap
        for offset, tap in enumerate(cubic_taps(frac_ref[2, rows, :])):
            high, low = split(tap)
            taps_ref[8 + offset, rows, :] = high.astype(F32)
            taps_ref[12 + offset, rows, :] = low.astype(F32)
        first = (z_ref[rows, :] + (NZ - 1)) & (NZ - 1)
        taps_ref[16, rows, :] = (first & 15).astype(F32)
        taps_ref[17, rows, :] = (first >> 4).astype(F32)
        return carry

    lax.fori_loop(0, tiles // 8, step, 0)


def window(start, taps, length):
    delta = lax.broadcasted_iota(jnp.int32, (length, PTS), 0) - start
    weights = jnp.where(delta == 0, taps[0], 0.0)
    for offset in range(1, 4):
        weights = jnp.where(delta == offset, taps[offset], weights)
    return weights


def column(row, taps_ref):
    low_place = taps_ref[16, row, :].astype(BF)
    run = taps_ref[17, row, :].astype(BF)
    taps = [taps_ref[8 + k, row, :].astype(BF) for k in range(8)]
    pair = []
    for part in range(2):
        delta = (lax.broadcasted_iota(jnp.int32, (16, PTS), 0) + 16 * part).astype(F32).astype(BF) - low_place
        high = low = jnp.zeros((16, PTS), BF)
        for k in range(4):
            hit = delta == k
            high = jnp.where(hit, taps[k], high)
            low = jnp.where(hit, taps[4 + k], low)
        pair.append((high, low))
    wide_run = jnp.broadcast_to(run, (16, PTS))
    zero = jnp.zeros((16, PTS), BF)
    highs, lows = [], []
    before = wide_run == NZ // 16 - 1
    for i in range(NZ // 16):
        here = wide_run == i
        highs.append(jnp.where(here, pair[0][0], jnp.where(before, pair[1][0], zero)))
        lows.append(jnp.where(here, pair[0][1], jnp.where(before, pair[1][1], zero)))
        before = here
    return jnp.concatenate(highs, 0), jnp.concatenate(lows, 0)


def spread_kernel(
    grid_ref, counts_ref, val_ref, frac_ref, xy_ref, z_ref, tz_ref, out_ref,
    taps_ref, pad_ref,
):
    tiles = val_ref.shape[0]
    fill_taps(frac_ref, z_ref, taps_ref)
    pad_ref[...] = jnp.zeros_like(pad_ref)
    slots = lax.broadcasted_iota(jnp.int32, (1, PTS), 1)

    def step(t, carry):
        row = pl.ds(t, 1)
        taps = [taps_ref[k, row, :] for k in range(8)]
        source = jnp.where(slots < counts_ref[t], val_ref[row, :], 0.0)
        wide_x = window(xy_ref[0, row, :], taps[0:4], 16)
        wide_y = window(xy_ref[1, row, :], [tap * source for tap in taps[4:8]], 16)
        plane = jnp.concatenate([wide_y[q : q + 1] * wide_x for q in range(BOX)], 0)
        high, low = split(plane)
        col = column(row, taps_ref)
        box = mm(
            jnp.concatenate([high, low, high], 1), jnp.concatenate([col[0], col[0], col[1]], 1), NT
        )
        g = grid_ref[t]
        gx = g // GROW
        gy = g - gx * GROW
        place = pl.ds(pl.multiple_of(gx * TILE, TILE), 16)
        for q in range(BOX):
            pad_ref[gy * TILE + q, place, :] += box[q * 16 : q * 16 + 16]
        return carry

    lax.fori_loop(0, tiles, step, 0, unroll=64)

    table = (tz_ref[:NZ], tz_ref[NZ:])

    def put(rows, first, second):
        turned = mm3(table, split(rows), NT)
        a, b = swap(turned[:DEVS], turned[DEVS:])
        out_ref[pl.ds(first, DEVS, stride=BLK), :] = a
        if second is not None:
            out_ref[pl.ds(second, DEVS, stride=BLK), :] = b

    for pair in range(SY // 2):
        y = 2 * pair
        rows = jnp.concatenate([pad_ref[y, 1:65, :], pad_ref[y + 1, 1:65, :]], 0)
        put(rows, y, y + 1 if y + 1 < EY else None)
    edges = [
        jnp.concatenate([pad_ref[:, at, :], jnp.zeros((64 - SY, NZ), F32)], 0) for at, _ in HALO
    ]
    put(jnp.concatenate([edges[0], edges[1]], 0), EY, EY + 1)
    put(jnp.concatenate([edges[2], jnp.zeros((64, NZ), F32)], 0), EY + 2, EY + 3)
    out_ref[pl.ds(BLK - 1, DEVS, stride=BLK), :] = jnp.zeros((DEVS, 128), F32)


def filter_kernel(
    dev_ref, rz_ref, rx_ref, ry_ref, in_ref, x_hbm, y_hbm, yt_hbm, ey_hbm, out_ref,
    x_ref, y_ref, yt_ref, ey_ref, th_ref, tl_ref, eh_ref, el_ref, wh_ref, wl_ref, uh_ref, ul_ref, ry2_ref, sems,
):
    copies = [
        pltpu.make_async_copy(source, target, sems.at[n])
        for n, (source, target) in enumerate(
            ((y_hbm, y_ref), (ey_hbm, ey_ref), (x_hbm, x_ref), (yt_hbm, yt_ref))
        )
    ]
    for copy in copies:
        copy.start()
    rows = RY * BLK
    half = NX // 2
    ry2_ref[...] = jnp.transpose(jnp.broadcast_to(ry_ref[...], (128, NY)))

    copies[0].wait()
    for j in range(RX // 4):
        sides = []
        for pair in (j, j + RX // 4):
            odd = []
            for parity in range(2):
                part = split(
                    jnp.concatenate(
                        [in_ref[pl.ds((2 * pair + n) * rows + parity, rows // 2, stride=2), :] for n in range(2)], 1
                    )
                )
                odd.append(mm3((y_ref[0, parity], y_ref[1, parity]), part))
            turned = (odd[1] + odd[0], odd[1] - odd[0])
            sides.append([swap(t[:, :128], t[:, 128:]) for t in turned])
        for k in range(2):
            at = slice(half * k, half * (k + 1))
            for z in range(2):
                first, second = sides[0][k][z], sides[1][k][z]
                for n, part in enumerate((first + second, first - second)):
                    lanes = slice(half * n + 128 * j, half * n + 128 * (j + 1))
                    high, low = split(part)
                    th_ref[z, at, lanes] = high
                    tl_ref[z, at, lanes] = low

    parts = ([], [])
    for j in range(RY // 2):
        load = [
            jnp.concatenate(
                [
                    in_ref[pl.ds((2 * j + i) * BLK + EY + col, RX, stride=rows), :]
                    for col in range(3)
                ],
                0,
            )
            for i in range(2)
        ]
        a, b = swap(load[0], load[1])
        parts[0].append(a)
        parts[1].append(b)
    edge = split(jnp.concatenate([jnp.concatenate(p, 1) for p in parts], 0))
    copies[1].wait()
    for i in range(2):
        at = slice(half * i, half * (i + 1))
        high, low = split(mm3((ey_ref[0, at, :], ey_ref[1, at, :]), edge, NT))
        eh_ref[at, :] = high
        el_ref[at, :] = low

    copies[2].wait()
    dev = dev_ref[0]
    scale = 4.0 / (NX * NY * NZ)
    table = [
        tuple(x_ref[part, :half, half * n : half * (n + 1)] for part in range(2)) for n in range(2)
    ]
    for i in range(half // CHUNK):
        fields = []
        for k in range(2):
            at = slice(half * k + CHUNK * i, half * k + CHUNK * (i + 1))
            back = []
            for z in range(2):
                rate = 1.0 + rz_ref[dev + z * DEVS]
                sums = []
                for n in range(2):
                    lanes = slice(half * n, half * (n + 1))
                    ends = slice(EX2 + 48 * z, EX2 + 48 * z + 48)
                    coeffs = mm3((th_ref[z, at, lanes], tl_ref[z, at, lanes]), table[n]) + mm3(
                        (eh_ref[at, :], el_ref[at, :]), (x_ref[0, ends, lanes], x_ref[1, ends, lanes])
                    )
                    weighted = []
                    for q in range(2):
                        cut = slice(half * n + 128 * q, half * n + 128 * (q + 1))
                        denom = ry2_ref[at, :] + (rx_ref[:, cut] + rate)
                        weighted.append(coeffs[:, 128 * q : 128 * (q + 1)] * (scale / (denom * denom)))
                    weighted = split(jnp.concatenate(weighted, 1))
                    wh_ref[z, at, lanes] = weighted[0]
                    wl_ref[z, at, lanes] = weighted[1]
                    sums.append(mm3(weighted, table[n], NT))
                back.append((sums[0] + sums[1], sums[0] - sums[1]))
            fields.append(back)
        for side in range(2):
            for q in range(2):
                lanes = slice(128 * q, 128 * (q + 1))
                low_k = swap(fields[0][0][side][:, lanes], fields[0][1][side][:, lanes])
                high_k = swap(fields[1][0][side][:, lanes], fields[1][1][side][:, lanes])
                for n in range(2):
                    block = 4 * side + 2 * q + n
                    for parity, value in enumerate((low_k[n] + high_k[n], low_k[n] - high_k[n])):
                        high, low = split(value)
                        uh_ref[parity, CHUNK * i : CHUNK * (i + 1), 128 * block : 128 * (block + 1)] = high
                        ul_ref[parity, CHUNK * i : CHUNK * (i + 1), 128 * block : 128 * (block + 1)] = low

    copies[3].wait()
    for j in range(RX // 2):
        lanes = slice(256 * j, 256 * (j + 1))
        for parity in range(2):
            field = (uh_ref[1 - parity, :, lanes], ul_ref[1 - parity, :, lanes])
            turned = mm3((yt_ref[0, parity], yt_ref[1, parity]), field)
            for n in range(2):
                out_ref[pl.ds((2 * j + n) * rows + parity, rows // 2, stride=2), :] = turned[
                    :, 128 * n : 128 * (n + 1)
                ]

    ends = slice(EX, EX + 24)
    tall = split(
        jnp.concatenate(
            [
                mm3((x_ref[0, ends, :], x_ref[1, ends, :]), (wh_ref[z], wl_ref[z]), NT)
                for z in range(2)
            ],
            0,
        )
    )
    for j in range(RY // 2):
        lanes = slice(128 * j, 128 * (j + 1))
        wide = mm3(tall, (ey_ref[0, :, lanes], ey_ref[1, :, lanes]))
        for n, part in enumerate(swap(wide[:24], wide[24:])):
            for col in range(3):
                out_ref[pl.ds((2 * j + n) * BLK + EY + col, RX, stride=rows), :] = part[
                    8 * col : 8 * col + 8
                ]


def sample_kernel(
    grid_ref, counts_ref, val_ref, noise_ref, frac_ref, xy_ref, z_ref, in_ref, tz_ref, out_ref,
    taps_ref, pad_ref, boxh_ref, boxl_ref,
):
    tiles = val_ref.shape[0]
    fill_taps(frac_ref, z_ref, taps_ref)
    table = (tz_ref[:NZ], tz_ref[NZ:])

    def get(first, second):
        a = in_ref[pl.ds(first, DEVS, stride=BLK), :]
        b = in_ref[pl.ds(second, DEVS, stride=BLK), :]
        turned = jnp.concatenate(swap(a, b), 0)
        return mm3(split(jnp.transpose(turned)), table)

    for pair in range(SY // 2):
        y = 2 * pair
        rows = get(y, y + 1)
        pad_ref[y, 1:65, :] = rows[:64]
        pad_ref[y + 1, 1:65, :] = rows[64:]
    for first, at in ((EY, (0, 1)), (EY + 2, (2,))):
        rows = get(first, first + 1)
        for n, col in enumerate(at):
            pad_ref[:, HALO[col][0], :] = rows[64 * n : 64 * n + SY]
    pad_ref[:, 67:72, :] = jnp.zeros((SY, 5, NZ), F32)
    for gx in range(BX // TILE):
        for y in range(SY):
            high, low = split(pad_ref[y, TILE * gx : TILE * gx + 16, :])
            boxh_ref[gx, y] = high
            boxl_ref[gx, y] = low

    slots = lax.broadcasted_iota(jnp.int32, (1, PTS), 1)

    def step(t, carry):
        row = pl.ds(t, 1)
        taps = [taps_ref[k, row, :] for k in range(8)]
        wide_x = window(xy_ref[0, row, :], taps[0:4], 16)
        wide_y = window(xy_ref[1, row, :], taps[4:8], 16)
        col = column(row, taps_ref)
        g = grid_ref[t]
        gx = g // GROW
        gy = g - gx * GROW
        place = pl.ds(gy * TILE, BOX)
        high = boxh_ref[gx, place].reshape(BOX * 16, NZ)
        low = boxl_ref[gx, place].reshape(BOX * 16, NZ)
        along = mm(jnp.concatenate([high, low], 0), jnp.concatenate(col, 1))
        along = along[: BOX * 16, :PTS] + along[: BOX * 16, PTS:] + along[BOX * 16 :, :PTS]
        total = wide_y[0:1] * along[0:16]
        for q in range(1, BOX):
            total = total + wide_y[q : q + 1] * along[16 * q : 16 * q + 16]
        sampled = jnp.sum(total * wide_x, axis=0, keepdims=True)
        out_ref[row, :] = jnp.where(
            slots < counts_ref[t], noise_ref[row, :] * val_ref[row, :] + sampled, 0.0
        )
        return carry

    lax.fori_loop(0, tiles, step, 0, unroll=64)


def body(values, noise, fractions, cell_xy, cell_z, tile_grid, counts, rate_x, rate_y, rate_z):
    tiles = values.shape[0]
    tab = {name: jnp.asarray(table) for name, table in tables().items()}
    vmem = pl.BlockSpec(memory_space=pltpu.VMEM)
    smem = pl.BlockSpec(memory_space=pltpu.SMEM)
    large = pltpu.CompilerParams(vmem_limit_bytes=56 << 20)
    limit = pltpu.CompilerParams(vmem_limit_bytes=32 << 20)
    exchange = jax.ShapeDtypeStruct((DEVS * BLK, 128), F32)

    sent = pl.pallas_call(
        spread_kernel,
        out_shape=exchange,
        in_specs=[smem] * 2 + [vmem] * 5,
        out_specs=vmem,
        scratch_shapes=[pltpu.VMEM((18, tiles, PTS), F32), pltpu.VMEM((SY, SX, NZ), F32)],
        compiler_params=large,
    )(tile_grid, counts, values, fractions, cell_xy, cell_z, tab["z"])

    def regroup(array):
        array = array.reshape(DEVS, BLK, 128)
        array = lax.all_to_all(array, ("gx", "gy"), split_axis=0, concat_axis=0, tiled=True)
        return array.reshape(DEVS * BLK, 128)

    planes = regroup(sent)
    dev = (lax.axis_index("gx") * RY + lax.axis_index("gy")).astype(jnp.int32).reshape(1)
    by_parity = rate_x.reshape(NX // 2, 2).T.reshape(1, NX)
    hbm = pl.BlockSpec(memory_space=pltpu.HBM)
    names = ("x", "y", "yt", "ey")
    filtered = pl.pallas_call(
        filter_kernel,
        out_shape=exchange,
        in_specs=[smem] * 2 + [vmem] * 3 + [hbm] * 4,
        out_specs=vmem,
        scratch_shapes=[pltpu.VMEM(tab[name].shape, BF) for name in names]
        + [
            pltpu.VMEM((2, NY, NX), BF),
            pltpu.VMEM((2, NY, NX), BF),
            pltpu.VMEM((NY, 48), BF),
            pltpu.VMEM((NY, 48), BF),
            pltpu.VMEM((2, NY, NX), BF),
            pltpu.VMEM((2, NY, NX), BF),
            pltpu.VMEM((2, NY // 2, 2 * NX), BF),
            pltpu.VMEM((2, NY // 2, 2 * NX), BF),
            pltpu.VMEM((NY, 128), F32),
            pltpu.SemaphoreType.DMA((4,)),
        ],
        compiler_params=limit,
    )(dev, rate_z, by_parity, rate_y.reshape(1, NY), planes, *[tab[name] for name in names])
    smooth = regroup(filtered)

    return pl.pallas_call(
        sample_kernel,
        out_shape=jax.ShapeDtypeStruct((tiles, PTS), F32),
        in_specs=[smem] * 2 + [vmem] * 7,
        out_specs=vmem,
        scratch_shapes=[
            pltpu.VMEM((18, tiles, PTS), F32),
            pltpu.VMEM((SY, SX, NZ), F32),
            pltpu.VMEM((BX // TILE, SY, 16, NZ), BF),
            pltpu.VMEM((BX // TILE, SY, 16, NZ), BF),
        ],
        compiler_params=limit,
    )(tile_grid, counts, values, noise, fractions, cell_xy, cell_z, smooth, tab["z"])


def solution(mesh):
    points = P(("gx", "gy"), None)
    triple = P(None, ("gx", "gy"), None)
    flat = P(("gx", "gy"))
    in_specs = (points, points, triple, triple, points, flat, flat, P(), P(), P())
    return jax.shard_map(body, mesh=mesh, in_specs=in_specs, out_specs=points, check_vma=False)
```

```python
import math

import jax
import jax.numpy as jnp
import ml_dtypes
import numpy as np
from jax import lax
from jax.experimental import pallas as pl
from jax.experimental.pallas import tpu as pltpu
from jax.sharding import PartitionSpec as P

NX, NY, NZ = 512, 512, 256
TILE = 8
PTS = 128
RX, RY = 8, 16
DEVS = RX * RY
BX, BY = NX // RX, NY // RY
GROW = BY // TILE
EY = BY + 3
SY, SX = 36, 72
BOX = 11
BLK = 40
HALO = ((0, -1), (65, 64), (66, 65))
CHUNK = 128

BF = jnp.bfloat16
F32 = jnp.float32
NN = (((1,), (0,)), ((), ()))
NT = (((1,), (1,)), ((), ()))
TN = (((0,), (0,)), ((), ()))


def halves(table):
    table = np.asarray(table, np.float32)
    high = table.astype(ml_dtypes.bfloat16)
    low = (table - high.astype(np.float32)).astype(ml_dtypes.bfloat16)
    return high, low


def cas(rows, columns, length):
    phase = np.outer(np.asarray(rows, np.int64), np.asarray(columns, np.int64)) % length
    angle = phase * (2.0 * math.pi / length)
    return np.cos(angle) + np.sin(angle)


def tables():
    half = np.arange(NX // 2)
    line = np.arange(EY) - 1
    full_y = cas(np.arange(NY), (np.arange(RY)[:, None] * BY + line[None, :]).reshape(-1) % NY, NY)
    full_y = full_y.reshape(NY, RY, EY)
    rows_y = np.zeros((NY // 2, RY, BLK))
    rows_y[:, :, :EY] = full_y[: NY // 2]
    rows_y = rows_y.reshape(NY // 2, RY * BLK // 2, 2)
    edge_y = np.zeros((NY, RY, 64))
    edge_y[:, :, :EY] = full_y
    edge_y = edge_y.reshape(NY, RY * 64)
    order = np.concatenate([2 * half, 2 * half + 1])
    edge_x = cas(np.concatenate([np.arange(RX) * BX + offset for _, offset in HALO]) % NX, order, NX)
    edge_two = np.zeros((2, 48, NX))
    edge_two[0, :24] = edge_x
    edge_two[1, 24:] = edge_x
    table_x = np.concatenate([cas(half, 2 * half, NX), cas(half, 2 * half + 1, NX)], 1)
    wide = np.concatenate([table_x, edge_two.reshape(96, NX), edge_x, np.zeros((8, NX))])
    return {
        "z": np.concatenate(halves(cas(np.arange(NZ), np.arange(NZ), NZ))),
        "x": np.stack(halves(wide)),
        "ey": np.stack(halves(np.concatenate([edge_y, rows_y.transpose(2, 0, 1).reshape(NY, -1)], 1))),
    }


EX2 = NX // 2
EX = EX2 + 96
EDGE = RY * 64


def split(value):
    high = value.astype(BF)
    return high, (value - high.astype(F32)).astype(BF)


def mm(a, b, dims=NN):
    return lax.dot_general(a, b, dims, preferred_element_type=F32)


def mm3(a, b, dims=NN):
    return mm(a[0], b[0], dims) + (mm(a[0], b[1], dims) + mm(a[1], b[0], dims))


def cubic_taps(fraction):
    square = fraction * fraction
    cubed = square * fraction
    return (
        -0.5 * cubed + square - 0.5 * fraction,
        1.5 * cubed - 2.5 * square + 1.0,
        -1.5 * cubed + 2.0 * square + 0.5 * fraction,
        0.5 * cubed - 0.5 * square,
    )


def low_lanes(shape):
    return lax.broadcasted_iota(jnp.int32, shape, 1) < 64


def swap(a, b):
    low = low_lanes(a.shape)
    return (
        jnp.where(low, a, pltpu.roll(b, 64, 1)),
        jnp.where(low, pltpu.roll(a, 64, 1), b),
    )


def fill_taps(frac_ref, z_ref, taps_ref):
    tiles = frac_ref.shape[1]

    def step(i, carry):
        rows = pl.ds(pl.multiple_of(i * 8, 8), 8)
        for axis in range(2):
            for offset, tap in enumerate(cubic_taps(frac_ref[axis, rows, :])):
                taps_ref[axis * 4 + offset, rows, :] = tap
        for offset, tap in enumerate(cubic_taps(frac_ref[2, rows, :])):
            high, low = split(tap)
            taps_ref[8 + offset, rows, :] = high.astype(F32)
            taps_ref[12 + offset, rows, :] = low.astype(F32)
        first = (z_ref[rows, :] + (NZ - 1)) & (NZ - 1)
        taps_ref[16, rows, :] = (first & 15).astype(F32)
        taps_ref[17, rows, :] = (first >> 4).astype(F32)
        return carry

    lax.fori_loop(0, tiles // 8, step, 0)


def window(start, taps, length):
    delta = lax.broadcasted_iota(jnp.int32, (length, PTS), 0) - start
    weights = jnp.where(delta == 0, taps[0], 0.0)
    for offset in range(1, 4):
        weights = jnp.where(delta == offset, taps[offset], weights)
    return weights


def column(row, taps_ref):
    low_place = taps_ref[16, row, :].astype(BF)
    run = taps_ref[17, row, :].astype(BF)
    taps = [taps_ref[8 + k, row, :].astype(BF) for k in range(8)]
    pair = []
    for part in range(2):
        delta = (lax.broadcasted_iota(jnp.int32, (16, PTS), 0) + 16 * part).astype(F32).astype(BF) - low_place
        high = low = jnp.zeros((16, PTS), BF)
        for k in range(4):
            hit = delta == k
            high = jnp.where(hit, taps[k], high)
            low = jnp.where(hit, taps[4 + k], low)
        pair.append((high, low))
    wide_run = jnp.broadcast_to(run, (16, PTS))
    zero = jnp.zeros((16, PTS), BF)
    highs, lows = [], []
    before = wide_run == NZ // 16 - 1
    for i in range(NZ // 16):
        here = wide_run == i
        highs.append(jnp.where(here, pair[0][0], jnp.where(before, pair[1][0], zero)))
        lows.append(jnp.where(here, pair[0][1], jnp.where(before, pair[1][1], zero)))
        before = here
    return jnp.concatenate(highs, 0), jnp.concatenate(lows, 0)


def spread_kernel(
    grid_ref, counts_ref, val_ref, frac_ref, xy_ref, z_ref, tz_ref, out_ref,
    taps_ref, pad_ref,
):
    tiles = val_ref.shape[0]
    fill_taps(frac_ref, z_ref, taps_ref)
    pad_ref[...] = jnp.zeros_like(pad_ref)
    slots = lax.broadcasted_iota(jnp.int32, (1, PTS), 1)

    def step(t, carry):
        row = pl.ds(t, 1)
        taps = [taps_ref[k, row, :] for k in range(8)]
        source = jnp.where(slots < counts_ref[t], val_ref[row, :], 0.0)
        wide_x = window(xy_ref[0, row, :], taps[0:4], 16)
        wide_y = window(xy_ref[1, row, :], [tap * source for tap in taps[4:8]], 16)
        plane = jnp.concatenate([wide_y[q : q + 1] * wide_x for q in range(BOX)], 0)
        high, low = split(plane)
        col = column(row, taps_ref)
        box = mm(
            jnp.concatenate([high, low, high], 1), jnp.concatenate([col[0], col[0], col[1]], 1), NT
        )
        g = grid_ref[t]
        gx = g // GROW
        gy = g - gx * GROW
        place = pl.ds(pl.multiple_of(gx * TILE, TILE), 16)
        for q in range(BOX):
            pad_ref[gy * TILE + q, place, :] += box[q * 16 : q * 16 + 16]
        return carry

    lax.fori_loop(0, tiles, step, 0, unroll=64)

    table = (tz_ref[:NZ], tz_ref[NZ:])

    def put(blocks, first, last):
        turned = mm3(table, split(jnp.concatenate(blocks, 0)), NT)
        for pair in range(2):
            lanes = slice(128 * pair, 128 * (pair + 1))
            for n, part in enumerate(swap(turned[:DEVS, lanes], turned[DEVS:, lanes])):
                if first + 2 * pair + n < last:
                    out_ref[pl.ds(first + 2 * pair + n, DEVS, stride=BLK), :] = part

    for first in range(0, SY, 4):
        put([pad_ref[first + n, 1:65, :] for n in range(4)], first, EY)
    edges = [
        jnp.concatenate([pad_ref[:, at, :], jnp.zeros((64 - SY, NZ), F32)], 0) for at, _ in HALO
    ]
    put(edges + [jnp.zeros((64, NZ), F32)], EY, EY + 4)
    out_ref[pl.ds(BLK - 1, DEVS, stride=BLK), :] = jnp.zeros((DEVS, 128), F32)


def filter_kernel(
    dev_ref, rz_ref, rx_ref, ry_ref, in_ref, x_ref, ey_ref, out_ref,
    th_ref, tl_ref, eh_ref, el_ref, wh_ref, wl_ref, uh_ref, ul_ref, ry2_ref,
):
    rows = RY * BLK
    half = NX // 2
    table_y = [
        tuple(ey_ref[part, half * p : half * (p + 1), EDGE:] for part in range(2)) for p in range(2)
    ]
    ry2_ref[...] = jnp.transpose(jnp.broadcast_to(ry_ref[...], (128, NY)))

    for j in range(RX // 4):
        sides = []
        for pair in (j, j + RX // 4):
            odd = []
            for parity in range(2):
                part = split(
                    jnp.concatenate(
                        [in_ref[pl.ds((2 * pair + n) * rows + parity, rows // 2, stride=2), :] for n in range(2)], 1
                    )
                )
                odd.append(mm3(table_y[parity], part))
            turned = (odd[1] + odd[0], odd[1] - odd[0])
            sides.append([swap(t[:, :128], t[:, 128:]) for t in turned])
        for k in range(2):
            at = slice(half * k, half * (k + 1))
            for z in range(2):
                first, second = sides[0][k][z], sides[1][k][z]
                for n, part in enumerate((first + second, first - second)):
                    lanes = slice(half * n + 128 * j, half * n + 128 * (j + 1))
                    high, low = split(part)
                    th_ref[z, at, lanes] = high
                    tl_ref[z, at, lanes] = low

    parts = ([], [])
    for j in range(RY // 2):
        load = [
            jnp.concatenate(
                [
                    in_ref[pl.ds((2 * j + i) * BLK + EY + col, RX, stride=rows), :]
                    for col in range(3)
                ],
                0,
            )
            for i in range(2)
        ]
        a, b = swap(load[0], load[1])
        parts[0].append(a)
        parts[1].append(b)
    edge = split(jnp.concatenate([jnp.concatenate(p, 1) for p in parts], 0))
    for i in range(2):
        at = slice(half * i, half * (i + 1))
        high, low = split(mm3((ey_ref[0, at, :EDGE], ey_ref[1, at, :EDGE]), edge, NT))
        eh_ref[at, :] = high
        el_ref[at, :] = low

    dev = dev_ref[0]
    scale = 4.0 / (NX * NY * NZ)
    table = [
        tuple(x_ref[part, :half, half * n : half * (n + 1)] for part in range(2)) for n in range(2)
    ]
    for i in range(half // CHUNK):
        fields = []
        for k in range(2):
            at = slice(half * k + CHUNK * i, half * k + CHUNK * (i + 1))
            back = []
            for z in range(2):
                rate = 1.0 + rz_ref[dev + z * DEVS]
                sums = []
                for n in range(2):
                    lanes = slice(half * n, half * (n + 1))
                    ends = slice(EX2 + 48 * z, EX2 + 48 * z + 48)
                    coeffs = mm3((th_ref[z, at, lanes], tl_ref[z, at, lanes]), table[n]) + mm3(
                        (eh_ref[at, :], el_ref[at, :]), (x_ref[0, ends, lanes], x_ref[1, ends, lanes])
                    )
                    weighted = []
                    for q in range(2):
                        cut = slice(half * n + 128 * q, half * n + 128 * (q + 1))
                        denom = ry2_ref[at, :] + (rx_ref[:, cut] + rate)
                        weighted.append(coeffs[:, 128 * q : 128 * (q + 1)] * (scale / (denom * denom)))
                    weighted = split(jnp.concatenate(weighted, 1))
                    wh_ref[z, at, lanes] = weighted[0]
                    wl_ref[z, at, lanes] = weighted[1]
                    sums.append(mm3(weighted, table[n], NT))
                back.append((sums[0] + sums[1], sums[0] - sums[1]))
            fields.append(back)
        for side in range(2):
            for q in range(2):
                lanes = slice(128 * q, 128 * (q + 1))
                low_k = swap(fields[0][0][side][:, lanes], fields[0][1][side][:, lanes])
                high_k = swap(fields[1][0][side][:, lanes], fields[1][1][side][:, lanes])
                for n in range(2):
                    block = 4 * side + 2 * q + n
                    for parity, value in enumerate((low_k[n] + high_k[n], low_k[n] - high_k[n])):
                        high, low = split(value)
                        uh_ref[parity, CHUNK * i : CHUNK * (i + 1), 128 * block : 128 * (block + 1)] = high
                        ul_ref[parity, CHUNK * i : CHUNK * (i + 1), 128 * block : 128 * (block + 1)] = low

    for j in range(RX // 2):
        lanes = slice(256 * j, 256 * (j + 1))
        for parity in range(2):
            field = (uh_ref[1 - parity, :, lanes], ul_ref[1 - parity, :, lanes])
            turned = mm3(table_y[parity], field, TN)
            for n in range(2):
                out_ref[pl.ds((2 * j + n) * rows + parity, rows // 2, stride=2), :] = turned[
                    :, 128 * n : 128 * (n + 1)
                ]

    ends = slice(EX, EX + 24)
    tall = split(
        jnp.concatenate(
            [
                mm3((x_ref[0, ends, :], x_ref[1, ends, :]), (wh_ref[z], wl_ref[z]), NT)
                for z in range(2)
            ],
            0,
        )
    )
    for j in range(RY // 2):
        lanes = slice(128 * j, 128 * (j + 1))
        wide = mm3(tall, (ey_ref[0, :, lanes], ey_ref[1, :, lanes]))
        for n, part in enumerate(swap(wide[:24], wide[24:])):
            for col in range(3):
                out_ref[pl.ds((2 * j + n) * BLK + EY + col, RX, stride=rows), :] = part[
                    8 * col : 8 * col + 8
                ]


def sample_kernel(
    grid_ref, counts_ref, val_ref, noise_ref, frac_ref, xy_ref, z_ref, in_ref, tz_ref, out_ref,
    taps_ref, pad_ref, boxh_ref, boxl_ref,
):
    tiles = val_ref.shape[0]
    fill_taps(frac_ref, z_ref, taps_ref)
    table = (tz_ref[:NZ], tz_ref[NZ:])

    def get(first, second):
        a = in_ref[pl.ds(first, DEVS, stride=BLK), :]
        b = in_ref[pl.ds(second, DEVS, stride=BLK), :]
        turned = jnp.concatenate(swap(a, b), 0)
        return mm3(split(jnp.transpose(turned)), table)

    for pair in range(SY // 2):
        y = 2 * pair
        rows = get(y, y + 1)
        pad_ref[y, 1:65, :] = rows[:64]
        pad_ref[y + 1, 1:65, :] = rows[64:]
    for first, at in ((EY, (0, 1)), (EY + 2, (2,))):
        rows = get(first, first + 1)
        for n, col in enumerate(at):
            pad_ref[:, HALO[col][0], :] = rows[64 * n : 64 * n + SY]
    pad_ref[:, 67:72, :] = jnp.zeros((SY, 5, NZ), F32)
    for gx in range(BX // TILE):
        for y in range(SY):
            high, low = split(pad_ref[y, TILE * gx : TILE * gx + 16, :])
            boxh_ref[gx, y] = high
            boxl_ref[gx, y] = low

    slots = lax.broadcasted_iota(jnp.int32, (1, PTS), 1)

    def step(t, carry):
        row = pl.ds(t, 1)
        taps = [taps_ref[k, row, :] for k in range(8)]
        wide_x = window(xy_ref[0, row, :], taps[0:4], 16)
        wide_y = window(xy_ref[1, row, :], taps[4:8], 16)
        col = column(row, taps_ref)
        g = grid_ref[t]
        gx = g // GROW
        gy = g - gx * GROW
        place = pl.ds(gy * TILE, BOX)
        high = boxh_ref[gx, place].reshape(BOX * 16, NZ)
        low = boxl_ref[gx, place].reshape(BOX * 16, NZ)
        along = mm(jnp.concatenate([high, low], 0), jnp.concatenate(col, 1))
        along = along[: BOX * 16, :PTS] + along[: BOX * 16, PTS:] + along[BOX * 16 :, :PTS]
        total = wide_y[0:1] * along[0:16]
        for q in range(1, BOX):
            total = total + wide_y[q : q + 1] * along[16 * q : 16 * q + 16]
        sampled = jnp.sum(total * wide_x, axis=0, keepdims=True)
        out_ref[row, :] = jnp.where(
            slots < counts_ref[t], noise_ref[row, :] * val_ref[row, :] + sampled, 0.0
        )
        return carry

    lax.fori_loop(0, tiles, step, 0, unroll=64)


def body(values, noise, fractions, cell_xy, cell_z, tile_grid, counts, rate_x, rate_y, rate_z):
    tiles = values.shape[0]
    tab = {name: jnp.asarray(table) for name, table in tables().items()}
    vmem = pl.BlockSpec(memory_space=pltpu.VMEM)
    smem = pl.BlockSpec(memory_space=pltpu.SMEM)
    large = pltpu.CompilerParams(vmem_limit_bytes=56 << 20)
    limit = pltpu.CompilerParams(vmem_limit_bytes=32 << 20)
    exchange = jax.ShapeDtypeStruct((DEVS * BLK, 128), F32)

    sent = pl.pallas_call(
        spread_kernel,
        out_shape=exchange,
        in_specs=[smem] * 2 + [vmem] * 5,
        out_specs=vmem,
        scratch_shapes=[pltpu.VMEM((18, tiles, PTS), F32), pltpu.VMEM((SY, SX, NZ), F32)],
        compiler_params=large,
    )(tile_grid, counts, values, fractions, cell_xy, cell_z, tab["z"])

    def regroup(array):
        array = array.reshape(DEVS, BLK, 128)
        array = lax.all_to_all(array, ("gx", "gy"), split_axis=0, concat_axis=0, tiled=True)
        return array.reshape(DEVS * BLK, 128)

    planes = regroup(sent)
    dev = (lax.axis_index("gx") * RY + lax.axis_index("gy")).astype(jnp.int32).reshape(1)
    by_parity = rate_x.reshape(NX // 2, 2).T.reshape(1, NX)
    names = ("x", "ey")
    filtered = pl.pallas_call(
        filter_kernel,
        out_shape=exchange,
        in_specs=[smem] * 2 + [vmem] * 5,
        out_specs=vmem,
        scratch_shapes=[
            pltpu.VMEM((2, NY, NX), BF),
            pltpu.VMEM((2, NY, NX), BF),
            pltpu.VMEM((NY, 48), BF),
            pltpu.VMEM((NY, 48), BF),
            pltpu.VMEM((2, NY, NX), BF),
            pltpu.VMEM((2, NY, NX), BF),
            pltpu.VMEM((2, NY // 2, 2 * NX), BF),
            pltpu.VMEM((2, NY // 2, 2 * NX), BF),
            pltpu.VMEM((NY, 128), F32),
        ],
        compiler_params=limit,
    )(dev, rate_z, by_parity, rate_y.reshape(1, NY), planes, *[tab[name] for name in names])
    smooth = regroup(filtered)

    return pl.pallas_call(
        sample_kernel,
        out_shape=jax.ShapeDtypeStruct((tiles, PTS), F32),
        in_specs=[smem] * 2 + [vmem] * 7,
        out_specs=vmem,
        scratch_shapes=[
            pltpu.VMEM((18, tiles, PTS), F32),
            pltpu.VMEM((SY, SX, NZ), F32),
            pltpu.VMEM((BX // TILE, SY, 16, NZ), BF),
            pltpu.VMEM((BX // TILE, SY, 16, NZ), BF),
        ],
        compiler_params=limit,
    )(tile_grid, counts, values, noise, fractions, cell_xy, cell_z, smooth, tab["z"])


def solution(mesh):
    points = P(("gx", "gy"), None)
    triple = P(None, ("gx", "gy"), None)
    flat = P(("gx", "gy"))
    in_specs = (points, points, triple, triple, points, flat, flat, P(), P(), P())
    return jax.shard_map(body, mesh=mesh, in_specs=in_specs, out_specs=points, check_vma=False)
```

```python
import math

import jax
import jax.numpy as jnp
import ml_dtypes
import numpy as np
from jax import lax
from jax.experimental import pallas as pl
from jax.experimental.pallas import tpu as pltpu
from jax.sharding import PartitionSpec as P

NX, NY, NZ = 512, 512, 256
TILE = 8
PTS = 128
RX, RY = 8, 16
DEVS = RX * RY
BX, BY = NX // RX, NY // RY
GROW = BY // TILE
EY = BY + 3
SY, SX = 36, 72
BOX = 11
BLK = 40
HALO = ((0, -1), (65, 64), (66, 65))
CHUNK = 128

BF = jnp.bfloat16
F32 = jnp.float32
NN = (((1,), (0,)), ((), ()))
NT = (((1,), (1,)), ((), ()))
TN = (((0,), (0,)), ((), ()))


def halves(table):
    table = np.asarray(table, np.float32)
    high = table.astype(ml_dtypes.bfloat16)
    low = (table - high.astype(np.float32)).astype(ml_dtypes.bfloat16)
    return high, low


def cas(rows, columns, length):
    phase = np.outer(np.asarray(rows, np.int64), np.asarray(columns, np.int64)) % length
    angle = phase * (2.0 * math.pi / length)
    return np.cos(angle) + np.sin(angle)


def tables():
    half = np.arange(NX // 2)
    line = np.arange(EY) - 1
    full_y = cas(np.arange(NY), (np.arange(RY)[:, None] * BY + line[None, :]).reshape(-1) % NY, NY)
    full_y = full_y.reshape(NY, RY, EY)
    rows_y = np.zeros((NY // 2, RY, BLK))
    rows_y[:, :, :EY] = full_y[: NY // 2]
    rows_y = rows_y.reshape(NY // 2, RY * BLK // 2, 2)
    edge_y = np.zeros((NY, RY, 64))
    edge_y[:, :, :EY] = full_y
    edge_y = edge_y.reshape(NY, RY * 64)
    order = np.concatenate([2 * half, 2 * half + 1])
    edge_x = cas(np.concatenate([np.arange(RX) * BX + offset for _, offset in HALO]) % NX, order, NX)
    edge_two = np.zeros((2, 48, NX))
    edge_two[0, :24] = edge_x
    edge_two[1, 24:] = edge_x
    table_x = np.concatenate([cas(half, 2 * half, NX), cas(half, 2 * half + 1, NX)], 1)
    wide = np.concatenate([table_x, edge_two.reshape(96, NX), edge_x, np.zeros((8, NX))])
    return {
        "z": np.concatenate(halves(cas(np.arange(NZ), np.arange(NZ), NZ))),
        "x": np.stack(halves(wide)),
        "ey": np.stack(halves(np.concatenate([edge_y, rows_y.transpose(2, 0, 1).reshape(NY, -1)], 1))),
    }


EX2 = NX // 2
EX = EX2 + 96
EDGE = RY * 64


def split(value):
    high = value.astype(BF)
    return high, (value - high.astype(F32)).astype(BF)


def mm(a, b, dims=NN):
    return lax.dot_general(a, b, dims, preferred_element_type=F32)


def mm3(a, b, dims=NN):
    return mm(a[0], b[0], dims) + (mm(a[0], b[1], dims) + mm(a[1], b[0], dims))


def cubic_taps(fraction):
    square = fraction * fraction
    cubed = square * fraction
    return (
        -0.5 * cubed + square - 0.5 * fraction,
        1.5 * cubed - 2.5 * square + 1.0,
        -1.5 * cubed + 2.0 * square + 0.5 * fraction,
        0.5 * cubed - 0.5 * square,
    )


def low_lanes(shape):
    return lax.broadcasted_iota(jnp.int32, shape, 1) < 64


def swap(a, b):
    low = low_lanes(a.shape)
    return (
        jnp.where(low, a, pltpu.roll(b, 64, 1)),
        jnp.where(low, pltpu.roll(a, 64, 1), b),
    )


def fill_taps(frac_ref, z_ref, taps_ref):
    tiles = frac_ref.shape[1]

    def step(i, carry):
        rows = pl.ds(pl.multiple_of(i * 8, 8), 8)
        for axis in range(2):
            for offset, tap in enumerate(cubic_taps(frac_ref[axis, rows, :])):
                taps_ref[axis * 4 + offset, rows, :] = tap
        for offset, tap in enumerate(cubic_taps(frac_ref[2, rows, :])):
            high, low = split(tap)
            taps_ref[8 + offset, rows, :] = high.astype(F32)
            taps_ref[12 + offset, rows, :] = low.astype(F32)
        first = (z_ref[rows, :] + (NZ - 1)) & (NZ - 1)
        taps_ref[16, rows, :] = (first & 15).astype(F32)
        taps_ref[17, rows, :] = (first >> 4).astype(F32)
        return carry

    lax.fori_loop(0, tiles // 8, step, 0)


def window(start, taps, length):
    delta = lax.broadcasted_iota(jnp.int32, (length, PTS), 0) - start
    weights = jnp.where(delta == 0, taps[0], 0.0)
    for offset in range(1, 4):
        weights = jnp.where(delta == offset, taps[offset], weights)
    return weights


def column(row, taps_ref):
    low_place = taps_ref[16, row, :].astype(BF)
    run = taps_ref[17, row, :].astype(BF)
    taps = [taps_ref[8 + k, row, :].astype(BF) for k in range(8)]
    pair = []
    for part in range(2):
        delta = (lax.broadcasted_iota(jnp.int32, (16, PTS), 0) + 16 * part).astype(F32).astype(BF) - low_place
        high = low = jnp.zeros((16, PTS), BF)
        for k in range(4):
            hit = delta == k
            high = jnp.where(hit, taps[k], high)
            low = jnp.where(hit, taps[4 + k], low)
        pair.append((high, low))
    wide_run = jnp.broadcast_to(run, (16, PTS))
    zero = jnp.zeros((16, PTS), BF)
    highs, lows = [], []
    before = wide_run == NZ // 16 - 1
    for i in range(NZ // 16):
        here = wide_run == i
        highs.append(jnp.where(here, pair[0][0], jnp.where(before, pair[1][0], zero)))
        lows.append(jnp.where(here, pair[0][1], jnp.where(before, pair[1][1], zero)))
        before = here
    return jnp.concatenate(highs, 0), jnp.concatenate(lows, 0)


def spread_kernel(
    grid_ref, counts_ref, val_ref, frac_ref, xy_ref, z_ref, tz_ref, out_ref,
    taps_ref, pad_ref,
):
    tiles = val_ref.shape[0]
    fill_taps(frac_ref, z_ref, taps_ref)
    pad_ref[...] = jnp.zeros_like(pad_ref)
    slots = lax.broadcasted_iota(jnp.int32, (1, PTS), 1)

    def step(t, carry):
        row = pl.ds(t, 1)
        taps = [taps_ref[k, row, :] for k in range(8)]
        source = jnp.where(slots < counts_ref[t], val_ref[row, :], 0.0)
        wide_x = window(xy_ref[0, row, :], taps[0:4], 16)
        wide_y = window(xy_ref[1, row, :], [tap * source for tap in taps[4:8]], 16)
        plane = jnp.concatenate([wide_y[q : q + 1] * wide_x for q in range(BOX)], 0)
        high, low = split(plane)
        col = column(row, taps_ref)
        turned = [jnp.transpose(part) for part in col]
        box = mm(jnp.concatenate([high, low, high], 1), jnp.concatenate([turned[0], turned[0], turned[1]], 0))
        g = grid_ref[t]
        gx = g // GROW
        gy = g - gx * GROW
        place = pl.ds(pl.multiple_of(gx * TILE, TILE), 16)
        for q in range(BOX):
            pad_ref[gy * TILE + q, place, :] += box[q * 16 : q * 16 + 16]
        return carry

    lax.fori_loop(0, tiles, step, 0, unroll=64)

    table = (tz_ref[:NZ], tz_ref[NZ:])

    def put(blocks, first, last):
        turned = mm3(table, split(jnp.concatenate(blocks, 0)), NT)
        for pair in range(2):
            lanes = slice(128 * pair, 128 * (pair + 1))
            for n, part in enumerate(swap(turned[:DEVS, lanes], turned[DEVS:, lanes])):
                if first + 2 * pair + n < last:
                    out_ref[pl.ds(first + 2 * pair + n, DEVS, stride=BLK), :] = part

    for first in range(0, SY, 4):
        put([pad_ref[first + n, 1:65, :] for n in range(4)], first, EY)
    edges = [
        jnp.concatenate([pad_ref[:, at, :], jnp.zeros((64 - SY, NZ), F32)], 0) for at, _ in HALO
    ]
    put(edges + [jnp.zeros((64, NZ), F32)], EY, EY + 4)
    out_ref[pl.ds(BLK - 1, DEVS, stride=BLK), :] = jnp.zeros((DEVS, 128), F32)


def filter_kernel(
    dev_ref, rz_ref, rx_ref, ry_ref, in_ref, x_ref, ey_ref, out_ref,
    th_ref, tl_ref, eh_ref, el_ref, wh_ref, wl_ref, uh_ref, ul_ref, ry2_ref,
):
    rows = RY * BLK
    half = NX // 2
    table_y = [
        tuple(ey_ref[part, half * p : half * (p + 1), EDGE:] for part in range(2)) for p in range(2)
    ]
    ry2_ref[...] = jnp.transpose(jnp.broadcast_to(ry_ref[...], (128, NY)))

    for j in range(RX // 4):
        sides = []
        for pair in (j, j + RX // 4):
            odd = []
            for parity in range(2):
                part = split(
                    jnp.concatenate(
                        [in_ref[pl.ds((2 * pair + n) * rows + parity, rows // 2, stride=2), :] for n in range(2)], 1
                    )
                )
                odd.append(mm3(table_y[parity], part))
            turned = (odd[1] + odd[0], odd[1] - odd[0])
            sides.append([swap(t[:, :128], t[:, 128:]) for t in turned])
        for k in range(2):
            at = slice(half * k, half * (k + 1))
            for z in range(2):
                first, second = sides[0][k][z], sides[1][k][z]
                for n, part in enumerate((first + second, first - second)):
                    lanes = slice(half * n + 128 * j, half * n + 128 * (j + 1))
                    high, low = split(part)
                    th_ref[z, at, lanes] = high
                    tl_ref[z, at, lanes] = low

    parts = ([], [])
    for j in range(RY // 2):
        load = [
            jnp.concatenate(
                [
                    in_ref[pl.ds((2 * j + i) * BLK + EY + col, RX, stride=rows), :]
                    for col in range(3)
                ],
                0,
            )
            for i in range(2)
        ]
        a, b = swap(load[0], load[1])
        parts[0].append(a)
        parts[1].append(b)
    edge = split(jnp.concatenate([jnp.concatenate(p, 1) for p in parts], 0))
    for i in range(2):
        at = slice(half * i, half * (i + 1))
        high, low = split(mm3((ey_ref[0, at, :EDGE], ey_ref[1, at, :EDGE]), edge, NT))
        eh_ref[at, :] = high
        el_ref[at, :] = low

    dev = dev_ref[0]
    scale = 4.0 / (NX * NY * NZ)
    table = [
        tuple(x_ref[part, :half, half * n : half * (n + 1)] for part in range(2)) for n in range(2)
    ]
    for i in range(half // CHUNK):
        fields = []
        for k in range(2):
            at = slice(half * k + CHUNK * i, half * k + CHUNK * (i + 1))
            back = []
            for z in range(2):
                rate = 1.0 + rz_ref[dev + z * DEVS]
                sums = []
                for n in range(2):
                    lanes = slice(half * n, half * (n + 1))
                    ends = slice(EX2 + 48 * z, EX2 + 48 * z + 48)
                    coeffs = mm3((th_ref[z, at, lanes], tl_ref[z, at, lanes]), table[n]) + mm3(
                        (eh_ref[at, :], el_ref[at, :]), (x_ref[0, ends, lanes], x_ref[1, ends, lanes])
                    )
                    weighted = []
                    for q in range(2):
                        cut = slice(half * n + 128 * q, half * n + 128 * (q + 1))
                        denom = ry2_ref[at, :] + (rx_ref[:, cut] + rate)
                        weighted.append(coeffs[:, 128 * q : 128 * (q + 1)] * (scale / (denom * denom)))
                    weighted = split(jnp.concatenate(weighted, 1))
                    wh_ref[z, at, lanes] = weighted[0]
                    wl_ref[z, at, lanes] = weighted[1]
                    sums.append(mm3(weighted, table[n], NT))
                back.append((sums[0] + sums[1], sums[0] - sums[1]))
            fields.append(back)
        for side in range(2):
            for q in range(2):
                lanes = slice(128 * q, 128 * (q + 1))
                low_k = swap(fields[0][0][side][:, lanes], fields[0][1][side][:, lanes])
                high_k = swap(fields[1][0][side][:, lanes], fields[1][1][side][:, lanes])
                for n in range(2):
                    block = 4 * side + 2 * q + n
                    for parity, value in enumerate((low_k[n] + high_k[n], low_k[n] - high_k[n])):
                        high, low = split(value)
                        uh_ref[parity, CHUNK * i : CHUNK * (i + 1), 128 * block : 128 * (block + 1)] = high
                        ul_ref[parity, CHUNK * i : CHUNK * (i + 1), 128 * block : 128 * (block + 1)] = low

    for j in range(RX // 2):
        lanes = slice(256 * j, 256 * (j + 1))
        for parity in range(2):
            field = (uh_ref[1 - parity, :, lanes], ul_ref[1 - parity, :, lanes])
            turned = mm3(table_y[parity], field, TN)
            for n in range(2):
                out_ref[pl.ds((2 * j + n) * rows + parity, rows // 2, stride=2), :] = turned[
                    :, 128 * n : 128 * (n + 1)
                ]

    ends = slice(EX, EX + 24)
    tall = split(
        jnp.concatenate(
            [
                mm3((x_ref[0, ends, :], x_ref[1, ends, :]), (wh_ref[z], wl_ref[z]), NT)
                for z in range(2)
            ],
            0,
        )
    )
    for j in range(RY // 2):
        lanes = slice(128 * j, 128 * (j + 1))
        wide = mm3(tall, (ey_ref[0, :, lanes], ey_ref[1, :, lanes]))
        for n, part in enumerate(swap(wide[:24], wide[24:])):
            for col in range(3):
                out_ref[pl.ds((2 * j + n) * BLK + EY + col, RX, stride=rows), :] = part[
                    8 * col : 8 * col + 8
                ]


def sample_kernel(
    grid_ref, counts_ref, val_ref, noise_ref, frac_ref, xy_ref, z_ref, in_ref, tz_ref, out_ref,
    taps_ref, pad_ref, boxh_ref, boxl_ref,
):
    tiles = val_ref.shape[0]
    fill_taps(frac_ref, z_ref, taps_ref)
    table = (tz_ref[:NZ], tz_ref[NZ:])

    def get(first, second):
        a = in_ref[pl.ds(first, DEVS, stride=BLK), :]
        b = in_ref[pl.ds(second, DEVS, stride=BLK), :]
        turned = jnp.concatenate(swap(a, b), 0)
        return mm3(split(jnp.transpose(turned)), table)

    for pair in range(SY // 2):
        y = 2 * pair
        rows = get(y, y + 1)
        pad_ref[y, 1:65, :] = rows[:64]
        pad_ref[y + 1, 1:65, :] = rows[64:]
    for first, at in ((EY, (0, 1)), (EY + 2, (2,))):
        rows = get(first, first + 1)
        for n, col in enumerate(at):
            pad_ref[:, HALO[col][0], :] = rows[64 * n : 64 * n + SY]
    pad_ref[:, 67:72, :] = jnp.zeros((SY, 5, NZ), F32)
    for gx in range(BX // TILE):
        for y in range(SY):
            high, low = split(pad_ref[y, TILE * gx : TILE * gx + 16, :])
            boxh_ref[gx, y] = high
            boxl_ref[gx, y] = low

    slots = lax.broadcasted_iota(jnp.int32, (1, PTS), 1)

    def step(t, carry):
        row = pl.ds(t, 1)
        taps = [taps_ref[k, row, :] for k in range(8)]
        wide_x = window(xy_ref[0, row, :], taps[0:4], 16)
        wide_y = window(xy_ref[1, row, :], taps[4:8], 16)
        col = column(row, taps_ref)
        g = grid_ref[t]
        gx = g // GROW
        gy = g - gx * GROW
        place = pl.ds(gy * TILE, BOX)
        high = boxh_ref[gx, place].reshape(BOX * 16, NZ)
        low = boxl_ref[gx, place].reshape(BOX * 16, NZ)
        along = mm(jnp.concatenate([high, low], 0), jnp.concatenate(col, 1))
        along = along[: BOX * 16, :PTS] + along[: BOX * 16, PTS:] + along[BOX * 16 :, :PTS]
        total = wide_y[0:1] * along[0:16]
        for q in range(1, BOX):
            total = total + wide_y[q : q + 1] * along[16 * q : 16 * q + 16]
        sampled = jnp.sum(total * wide_x, axis=0, keepdims=True)
        out_ref[row, :] = jnp.where(
            slots < counts_ref[t], noise_ref[row, :] * val_ref[row, :] + sampled, 0.0
        )
        return carry

    lax.fori_loop(0, tiles, step, 0, unroll=64)


def body(values, noise, fractions, cell_xy, cell_z, tile_grid, counts, rate_x, rate_y, rate_z):
    tiles = values.shape[0]
    tab = {name: jnp.asarray(table) for name, table in tables().items()}
    vmem = pl.BlockSpec(memory_space=pltpu.VMEM)
    smem = pl.BlockSpec(memory_space=pltpu.SMEM)
    large = pltpu.CompilerParams(vmem_limit_bytes=56 << 20)
    limit = pltpu.CompilerParams(vmem_limit_bytes=32 << 20)
    exchange = jax.ShapeDtypeStruct((DEVS * BLK, 128), F32)

    sent = pl.pallas_call(
        spread_kernel,
        out_shape=exchange,
        in_specs=[smem] * 2 + [vmem] * 5,
        out_specs=vmem,
        scratch_shapes=[pltpu.VMEM((18, tiles, PTS), F32), pltpu.VMEM((SY, SX, NZ), F32)],
        compiler_params=large,
    )(tile_grid, counts, values, fractions, cell_xy, cell_z, tab["z"])

    def regroup(array):
        array = array.reshape(DEVS, BLK, 128)
        array = lax.all_to_all(array, ("gx", "gy"), split_axis=0, concat_axis=0, tiled=True)
        return array.reshape(DEVS * BLK, 128)

    planes = regroup(sent)
    dev = (lax.axis_index("gx") * RY + lax.axis_index("gy")).astype(jnp.int32).reshape(1)
    by_parity = rate_x.reshape(NX // 2, 2).T.reshape(1, NX)
    names = ("x", "ey")
    filtered = pl.pallas_call(
        filter_kernel,
        out_shape=exchange,
        in_specs=[smem] * 2 + [vmem] * 5,
        out_specs=vmem,
        scratch_shapes=[
            pltpu.VMEM((2, NY, NX), BF),
            pltpu.VMEM((2, NY, NX), BF),
            pltpu.VMEM((NY, 48), BF),
            pltpu.VMEM((NY, 48), BF),
            pltpu.VMEM((2, NY, NX), BF),
            pltpu.VMEM((2, NY, NX), BF),
            pltpu.VMEM((2, NY // 2, 2 * NX), BF),
            pltpu.VMEM((2, NY // 2, 2 * NX), BF),
            pltpu.VMEM((NY, 128), F32),
        ],
        compiler_params=limit,
    )(dev, rate_z, by_parity, rate_y.reshape(1, NY), planes, *[tab[name] for name in names])
    smooth = regroup(filtered)

    return pl.pallas_call(
        sample_kernel,
        out_shape=jax.ShapeDtypeStruct((tiles, PTS), F32),
        in_specs=[smem] * 2 + [vmem] * 7,
        out_specs=vmem,
        scratch_shapes=[
            pltpu.VMEM((18, tiles, PTS), F32),
            pltpu.VMEM((SY, SX, NZ), F32),
            pltpu.VMEM((BX // TILE, SY, 16, NZ), BF),
            pltpu.VMEM((BX // TILE, SY, 16, NZ), BF),
        ],
        compiler_params=limit,
    )(tile_grid, counts, values, noise, fractions, cell_xy, cell_z, smooth, tab["z"])


def solution(mesh):
    points = P(("gx", "gy"), None)
    triple = P(None, ("gx", "gy"), None)
    flat = P(("gx", "gy"))
    in_specs = (points, points, triple, triple, points, flat, flat, P(), P(), P())
    return jax.shard_map(body, mesh=mesh, in_specs=in_specs, out_specs=points, check_vma=False)
```

```python
import math

import jax
import jax.numpy as jnp
import ml_dtypes
import numpy as np
from jax import lax
from jax.experimental import pallas as pl
from jax.experimental.pallas import tpu as pltpu
from jax.sharding import PartitionSpec as P

NX, NY, NZ = 512, 512, 256
TILE = 8
PTS = 128
RX, RY = 8, 16
DEVS = RX * RY
BX, BY = NX // RX, NY // RY
GROW = BY // TILE
EY = BY + 3
SY, SX = 36, 72
BOX = 11
BLK = 40
HALO = ((0, -1), (65, 64), (66, 65))
CHUNK = 128

BF = jnp.bfloat16
F32 = jnp.float32
NN = (((1,), (0,)), ((), ()))
NT = (((1,), (1,)), ((), ()))
TN = (((0,), (0,)), ((), ()))


def halves(table):
    table = np.asarray(table, np.float32)
    high = table.astype(ml_dtypes.bfloat16)
    low = (table - high.astype(np.float32)).astype(ml_dtypes.bfloat16)
    return high, low


def cas(rows, columns, length):
    phase = np.outer(np.asarray(rows, np.int64), np.asarray(columns, np.int64)) % length
    angle = phase * (2.0 * math.pi / length)
    return np.cos(angle) + np.sin(angle)


def tables():
    half = np.arange(NX // 2)
    line = np.arange(EY) - 1
    full_y = cas(np.arange(NY), (np.arange(RY)[:, None] * BY + line[None, :]).reshape(-1) % NY, NY)
    full_y = full_y.reshape(NY, RY, EY)
    rows_y = np.zeros((NY // 2, RY, BLK))
    rows_y[:, :, :EY] = full_y[: NY // 2]
    rows_y = rows_y.reshape(NY // 2, RY * BLK // 2, 2)
    edge_y = np.zeros((NY, RY, 64))
    edge_y[:, :, :EY] = full_y
    edge_y = edge_y.reshape(NY, RY * 64)
    order = np.concatenate([2 * half, 2 * half + 1])
    edge_x = cas(np.concatenate([np.arange(RX) * BX + offset for _, offset in HALO]) % NX, order, NX)
    edge_two = np.zeros((2, 48, NX))
    edge_two[0, :24] = edge_x
    edge_two[1, 24:] = edge_x
    table_x = np.concatenate([cas(half, 2 * half, NX), cas(half, 2 * half + 1, NX)], 1)
    wide = np.concatenate([table_x, edge_two.reshape(96, NX), edge_x, np.zeros((8, NX))])
    return {
        "z": np.concatenate(halves(cas(np.arange(NZ), np.arange(NZ), NZ))),
        "x": np.stack(halves(wide)),
        "ey": np.stack(halves(np.concatenate([edge_y, rows_y.transpose(2, 0, 1).reshape(NY, -1)], 1))),
    }


EX2 = NX // 2
EX = EX2 + 96
EDGE = RY * 64


def split(value):
    high = value.astype(BF)
    return high, (value - high.astype(F32)).astype(BF)


def mm(a, b, dims=NN):
    return lax.dot_general(a, b, dims, preferred_element_type=F32)


def mm3(a, b, dims=NN):
    return mm(a[0], b[0], dims) + (mm(a[0], b[1], dims) + mm(a[1], b[0], dims))


def cubic_taps(fraction):
    square = fraction * fraction
    cubed = square * fraction
    return (
        -0.5 * cubed + square - 0.5 * fraction,
        1.5 * cubed - 2.5 * square + 1.0,
        -1.5 * cubed + 2.0 * square + 0.5 * fraction,
        0.5 * cubed - 0.5 * square,
    )


def low_lanes(shape):
    return lax.broadcasted_iota(jnp.int32, shape, 1) < 64


def swap(a, b):
    low = low_lanes(a.shape)
    return (
        jnp.where(low, a, pltpu.roll(b, 64, 1)),
        jnp.where(low, pltpu.roll(a, 64, 1), b),
    )


def fill_taps(frac_ref, z_ref, taps_ref):
    tiles = frac_ref.shape[1]

    def step(i, carry):
        rows = pl.ds(pl.multiple_of(i * 8, 8), 8)
        for axis in range(2):
            for offset, tap in enumerate(cubic_taps(frac_ref[axis, rows, :])):
                taps_ref[axis * 4 + offset, rows, :] = tap
        for offset, tap in enumerate(cubic_taps(frac_ref[2, rows, :])):
            high, low = split(tap)
            taps_ref[8 + offset, rows, :] = high.astype(F32)
            taps_ref[12 + offset, rows, :] = low.astype(F32)
        first = (z_ref[rows, :] + (NZ - 1)) & (NZ - 1)
        taps_ref[16, rows, :] = (first & 15).astype(F32)
        taps_ref[17, rows, :] = (first >> 4).astype(F32)
        return carry

    lax.fori_loop(0, tiles // 8, step, 0)


def window(start, taps, length):
    delta = lax.broadcasted_iota(jnp.int32, (length, PTS), 0) - start
    weights = jnp.where(delta == 0, taps[0], 0.0)
    for offset in range(1, 4):
        weights = jnp.where(delta == offset, taps[offset], weights)
    return weights


def column(row, taps_ref):
    low_place = taps_ref[16, row, :].astype(BF)
    run = taps_ref[17, row, :].astype(BF)
    taps = [taps_ref[8 + k, row, :].astype(BF) for k in range(8)]
    pair = []
    for part in range(2):
        delta = (lax.broadcasted_iota(jnp.int32, (16, PTS), 0) + 16 * part).astype(F32).astype(BF) - low_place
        high = low = jnp.zeros((16, PTS), BF)
        for k in range(4):
            hit = delta == k
            high = jnp.where(hit, taps[k], high)
            low = jnp.where(hit, taps[4 + k], low)
        pair.append((high, low))
    wide_run = jnp.broadcast_to(run, (16, PTS))
    zero = jnp.zeros((16, PTS), BF)
    highs, lows = [], []
    before = wide_run == NZ // 16 - 1
    for i in range(NZ // 16):
        here = wide_run == i
        highs.append(jnp.where(here, pair[0][0], jnp.where(before, pair[1][0], zero)))
        lows.append(jnp.where(here, pair[0][1], jnp.where(before, pair[1][1], zero)))
        before = here
    return jnp.concatenate(highs, 0), jnp.concatenate(lows, 0)


def spread_kernel(
    grid_ref, counts_ref, val_ref, frac_ref, xy_ref, z_ref, tz_ref, out_ref,
    taps_ref, pad_ref,
):
    tiles = val_ref.shape[0]
    fill_taps(frac_ref, z_ref, taps_ref)
    pad_ref[...] = jnp.zeros_like(pad_ref)
    slots = lax.broadcasted_iota(jnp.int32, (1, PTS), 1)

    def step(t, carry):
        row = pl.ds(t, 1)
        taps = [taps_ref[k, row, :] for k in range(8)]
        source = jnp.where(slots < counts_ref[t], val_ref[row, :], 0.0)
        wide_x = window(xy_ref[0, row, :], taps[0:4], 16)
        wide_y = window(xy_ref[1, row, :], [tap * source for tap in taps[4:8]], 16)
        plane = jnp.concatenate([wide_y[q : q + 1] * wide_x for q in range(BOX)], 0)
        high, low = split(plane)
        col = column(row, taps_ref)
        turned = [jnp.transpose(part) for part in col]
        box = mm(jnp.concatenate([high, low], 1), jnp.concatenate([turned[0], turned[0]], 0)) + mm(high, turned[1])
        g = grid_ref[t]
        gx = g // GROW
        gy = g - gx * GROW
        place = pl.ds(pl.multiple_of(gx * TILE, TILE), 16)
        for q in range(BOX):
            pad_ref[gy * TILE + q, place, :] += box[q * 16 : q * 16 + 16]
        return carry

    lax.fori_loop(0, tiles, step, 0, unroll=64)

    table = (tz_ref[:NZ], tz_ref[NZ:])

    def put(blocks, first, last):
        turned = mm3(table, split(jnp.concatenate(blocks, 0)), NT)
        for pair in range(2):
            lanes = slice(128 * pair, 128 * (pair + 1))
            for n, part in enumerate(swap(turned[:DEVS, lanes], turned[DEVS:, lanes])):
                if first + 2 * pair + n < last:
                    out_ref[pl.ds(first + 2 * pair + n, DEVS, stride=BLK), :] = part

    for first in range(0, SY, 4):
        put([pad_ref[first + n, 1:65, :] for n in range(4)], first, EY)
    edges = [
        jnp.concatenate([pad_ref[:, at, :], jnp.zeros((64 - SY, NZ), F32)], 0) for at, _ in HALO
    ]
    put(edges + [jnp.zeros((64, NZ), F32)], EY, EY + 4)
    out_ref[pl.ds(BLK - 1, DEVS, stride=BLK), :] = jnp.zeros((DEVS, 128), F32)


def filter_kernel(
    dev_ref, rz_ref, rx_ref, ry_ref, in_ref, x_ref, ey_ref, out_ref,
    th_ref, tl_ref, eh_ref, el_ref, wh_ref, wl_ref, uh_ref, ul_ref, ry2_ref,
):
    rows = RY * BLK
    half = NX // 2
    table_y = [
        tuple(ey_ref[part, half * p : half * (p + 1), EDGE:] for part in range(2)) for p in range(2)
    ]
    ry2_ref[...] = jnp.transpose(jnp.broadcast_to(ry_ref[...], (128, NY)))

    for j in range(RX // 4):
        sides = []
        for pair in (j, j + RX // 4):
            odd = []
            for parity in range(2):
                part = split(
                    jnp.concatenate(
                        [in_ref[pl.ds((2 * pair + n) * rows + parity, rows // 2, stride=2), :] for n in range(2)], 1
                    )
                )
                odd.append(mm3(table_y[parity], part))
            turned = (odd[1] + odd[0], odd[1] - odd[0])
            sides.append([swap(t[:, :128], t[:, 128:]) for t in turned])
        for k in range(2):
            at = slice(half * k, half * (k + 1))
            for z in range(2):
                first, second = sides[0][k][z], sides[1][k][z]
                for n, part in enumerate((first + second, first - second)):
                    lanes = slice(half * n + 128 * j, half * n + 128 * (j + 1))
                    high, low = split(part)
                    th_ref[z, at, lanes] = high
                    tl_ref[z, at, lanes] = low

    parts = ([], [])
    for j in range(RY // 2):
        load = [
            jnp.concatenate(
                [
                    in_ref[pl.ds((2 * j + i) * BLK + EY + col, RX, stride=rows), :]
                    for col in range(3)
                ],
                0,
            )
            for i in range(2)
        ]
        a, b = swap(load[0], load[1])
        parts[0].append(a)
        parts[1].append(b)
    edge = split(jnp.concatenate([jnp.concatenate(p, 1) for p in parts], 0))
    for i in range(2):
        at = slice(half * i, half * (i + 1))
        high, low = split(mm3((ey_ref[0, at, :EDGE], ey_ref[1, at, :EDGE]), edge, NT))
        eh_ref[at, :] = high
        el_ref[at, :] = low

    dev = dev_ref[0]
    scale = 4.0 / (NX * NY * NZ)
    table = [
        tuple(x_ref[part, :half, half * n : half * (n + 1)] for part in range(2)) for n in range(2)
    ]
    for i in range(half // CHUNK):
        fields = []
        for k in range(2):
            at = slice(half * k + CHUNK * i, half * k + CHUNK * (i + 1))
            back = []
            for z in range(2):
                rate = 1.0 + rz_ref[dev + z * DEVS]
                sums = []
                for n in range(2):
                    lanes = slice(half * n, half * (n + 1))
                    ends = slice(EX2 + 48 * z, EX2 + 48 * z + 48)
                    coeffs = mm3((th_ref[z, at, lanes], tl_ref[z, at, lanes]), table[n]) + mm3(
                        (eh_ref[at, :], el_ref[at, :]), (x_ref[0, ends, lanes], x_ref[1, ends, lanes])
                    )
                    weighted = []
                    for q in range(2):
                        cut = slice(half * n + 128 * q, half * n + 128 * (q + 1))
                        denom = ry2_ref[at, :] + (rx_ref[:, cut] + rate)
                        weighted.append(coeffs[:, 128 * q : 128 * (q + 1)] * (scale / (denom * denom)))
                    weighted = split(jnp.concatenate(weighted, 1))
                    wh_ref[z, at, lanes] = weighted[0]
                    wl_ref[z, at, lanes] = weighted[1]
                    sums.append(mm3(weighted, table[n], NT))
                back.append((sums[0] + sums[1], sums[0] - sums[1]))
            fields.append(back)
        for side in range(2):
            for q in range(2):
                lanes = slice(128 * q, 128 * (q + 1))
                low_k = swap(fields[0][0][side][:, lanes], fields[0][1][side][:, lanes])
                high_k = swap(fields[1][0][side][:, lanes], fields[1][1][side][:, lanes])
                for n in range(2):
                    block = 4 * side + 2 * q + n
                    for parity, value in enumerate((low_k[n] + high_k[n], low_k[n] - high_k[n])):
                        high, low = split(value)
                        uh_ref[parity, CHUNK * i : CHUNK * (i + 1), 128 * block : 128 * (block + 1)] = high
                        ul_ref[parity, CHUNK * i : CHUNK * (i + 1), 128 * block : 128 * (block + 1)] = low

    for j in range(RX // 2):
        lanes = slice(256 * j, 256 * (j + 1))
        for parity in range(2):
            field = (uh_ref[1 - parity, :, lanes], ul_ref[1 - parity, :, lanes])
            turned = mm3(table_y[parity], field, TN)
            for n in range(2):
                out_ref[pl.ds((2 * j + n) * rows + parity, rows // 2, stride=2), :] = turned[
                    :, 128 * n : 128 * (n + 1)
                ]

    ends = slice(EX, EX + 32)
    tall = split(
        jnp.concatenate(
            [
                mm3((x_ref[0, ends, :], x_ref[1, ends, :]), (wh_ref[z], wl_ref[z]), NT)[:24]
                for z in range(2)
            ],
            0,
        )
    )
    for j in range(RY // 2):
        lanes = slice(128 * j, 128 * (j + 1))
        wide = mm3(tall, (ey_ref[0, :, lanes], ey_ref[1, :, lanes]))
        for n, part in enumerate(swap(wide[:24], wide[24:])):
            for col in range(3):
                out_ref[pl.ds((2 * j + n) * BLK + EY + col, RX, stride=rows), :] = part[
                    8 * col : 8 * col + 8
                ]


def sample_kernel(
    grid_ref, counts_ref, val_ref, noise_ref, frac_ref, xy_ref, z_ref, in_ref, tz_ref, out_ref,
    taps_ref, pad_ref, boxh_ref, boxl_ref,
):
    tiles = val_ref.shape[0]
    fill_taps(frac_ref, z_ref, taps_ref)
    table = (tz_ref[:NZ], tz_ref[NZ:])

    def get(first, second):
        a = in_ref[pl.ds(first, DEVS, stride=BLK), :]
        b = in_ref[pl.ds(second, DEVS, stride=BLK), :]
        turned = jnp.concatenate(swap(a, b), 0)
        return mm3(split(jnp.transpose(turned)), table)

    for pair in range(SY // 2):
        y = 2 * pair
        rows = get(y, y + 1)
        pad_ref[y, 1:65, :] = rows[:64]
        pad_ref[y + 1, 1:65, :] = rows[64:]
    for first, at in ((EY, (0, 1)), (EY + 2, (2,))):
        rows = get(first, first + 1)
        for n, col in enumerate(at):
            pad_ref[:, HALO[col][0], :] = rows[64 * n : 64 * n + SY]
    pad_ref[:, 67:72, :] = jnp.zeros((SY, 5, NZ), F32)
    for gx in range(BX // TILE):
        for y in range(SY):
            high, low = split(pad_ref[y, TILE * gx : TILE * gx + 16, :])
            boxh_ref[gx, y] = high
            boxl_ref[gx, y] = low

    slots = lax.broadcasted_iota(jnp.int32, (1, PTS), 1)

    def step(t, carry):
        row = pl.ds(t, 1)
        taps = [taps_ref[k, row, :] for k in range(8)]
        wide_x = window(xy_ref[0, row, :], taps[0:4], 16)
        wide_y = window(xy_ref[1, row, :], taps[4:8], 16)
        col = column(row, taps_ref)
        g = grid_ref[t]
        gx = g // GROW
        gy = g - gx * GROW
        place = pl.ds(gy * TILE, BOX)
        high = boxh_ref[gx, place].reshape(BOX * 16, NZ)
        low = boxl_ref[gx, place].reshape(BOX * 16, NZ)
        along = mm(jnp.concatenate([high, low], 0), jnp.concatenate(col, 1))
        along = along[: BOX * 16, :PTS] + along[: BOX * 16, PTS:] + along[BOX * 16 :, :PTS]
        total = wide_y[0:1] * along[0:16]
        for q in range(1, BOX):
            total = total + wide_y[q : q + 1] * along[16 * q : 16 * q + 16]
        sampled = jnp.sum(total * wide_x, axis=0, keepdims=True)
        out_ref[row, :] = jnp.where(
            slots < counts_ref[t], noise_ref[row, :] * val_ref[row, :] + sampled, 0.0
        )
        return carry

    lax.fori_loop(0, tiles, step, 0, unroll=64)


def body(values, noise, fractions, cell_xy, cell_z, tile_grid, counts, rate_x, rate_y, rate_z):
    tiles = values.shape[0]
    tab = {name: jnp.asarray(table) for name, table in tables().items()}
    vmem = pl.BlockSpec(memory_space=pltpu.VMEM)
    smem = pl.BlockSpec(memory_space=pltpu.SMEM)
    large = pltpu.CompilerParams(vmem_limit_bytes=56 << 20)
    limit = pltpu.CompilerParams(vmem_limit_bytes=32 << 20)
    exchange = jax.ShapeDtypeStruct((DEVS * BLK, 128), F32)

    sent = pl.pallas_call(
        spread_kernel,
        out_shape=exchange,
        in_specs=[smem] * 2 + [vmem] * 5,
        out_specs=vmem,
        scratch_shapes=[pltpu.VMEM((18, tiles, PTS), F32), pltpu.VMEM((SY, SX, NZ), F32)],
        compiler_params=large,
    )(tile_grid, counts, values, fractions, cell_xy, cell_z, tab["z"])

    def regroup(array):
        array = array.reshape(DEVS, BLK, 128)
        array = lax.all_to_all(array, ("gx", "gy"), split_axis=0, concat_axis=0, tiled=True)
        return array.reshape(DEVS * BLK, 128)

    planes = regroup(sent)
    dev = (lax.axis_index("gx") * RY + lax.axis_index("gy")).astype(jnp.int32).reshape(1)
    by_parity = rate_x.reshape(NX // 2, 2).T.reshape(1, NX)
    names = ("x", "ey")
    filtered = pl.pallas_call(
        filter_kernel,
        out_shape=exchange,
        in_specs=[smem] * 2 + [vmem] * 5,
        out_specs=vmem,
        scratch_shapes=[
            pltpu.VMEM((2, NY, NX), BF),
            pltpu.VMEM((2, NY, NX), BF),
            pltpu.VMEM((NY, 48), BF),
            pltpu.VMEM((NY, 48), BF),
            pltpu.VMEM((2, NY, NX), BF),
            pltpu.VMEM((2, NY, NX), BF),
            pltpu.VMEM((2, NY // 2, 2 * NX), BF),
            pltpu.VMEM((2, NY // 2, 2 * NX), BF),
            pltpu.VMEM((NY, 128), F32),
        ],
        compiler_params=limit,
    )(dev, rate_z, by_parity, rate_y.reshape(1, NY), planes, *[tab[name] for name in names])
    smooth = regroup(filtered)

    return pl.pallas_call(
        sample_kernel,
        out_shape=jax.ShapeDtypeStruct((tiles, PTS), F32),
        in_specs=[smem] * 2 + [vmem] * 7,
        out_specs=vmem,
        scratch_shapes=[
            pltpu.VMEM((18, tiles, PTS), F32),
            pltpu.VMEM((SY, SX, NZ), F32),
            pltpu.VMEM((BX // TILE, SY, 16, NZ), BF),
            pltpu.VMEM((BX // TILE, SY, 16, NZ), BF),
        ],
        compiler_params=limit,
    )(tile_grid, counts, values, noise, fractions, cell_xy, cell_z, smooth, tab["z"])


def solution(mesh):
    points = P(("gx", "gy"), None)
    triple = P(None, ("gx", "gy"), None)
    flat = P(("gx", "gy"))
    in_specs = (points, points, triple, triple, points, flat, flat, P(), P(), P())
    return jax.shard_map(body, mesh=mesh, in_specs=in_specs, out_specs=points, check_vma=False)
```
